1024 devices in a mesh: seq: 128 (over y, z), inner: 8 (over x, core).
Axes of the slice: x: 4, y: 4, z: 32, core: 2. Of those that a mesh axis runs over, the one named last changes fastest.
Arguments:
- queries: bfloat16 [8, 16, 262144], P('inner', None, 'seq'), may hold values from -24 to 24
- key_states: bfloat16 [8, 16, 262144], P('inner', None, 'seq'), may hold values from -24 to 24
- value_states: bfloat16 [128, 25, 262144], P('inner', None, 'seq'), may hold values from -48 to 48
- fractional: float32 [3, 262144], P(None, 'seq'), may hold values from 0 to 1
- block_counts: int32 [1024], replicated, may hold values from 64 to 256
- neighbors: int32 [1024, 3], P('seq'), may hold values from 0 to 1023, as said below
- integer_wave_vectors: int32 [3, 2048], replicated, may hold values from -7 to 7, as said below
- charge_weight: bfloat16 [128, 16], P('inner'), may hold values from -0.5 to 0.5
Outputs:
- attention: bfloat16 [128, 25, 262144], P('inner', None, 'seq')
- potential: float32 [16, 262144], P(None, 'seq')
- forces: float32 [3, 262144], P(None, 'seq')
The draws below stay inside these ranges and needn't reach their ends.
Inputs may be any that keep to these rules, and one draw needn't show every extreme that they name: `neighbors`: row g lists 3 different blocks from g - 2 to g + 2 that lie in the grid, g itself among them. `integer_wave_vectors`: no column is all zeros.
All inputs are finite; a program needn't handle non-finite values.
Results may differ from the reference program's by a relative error of at most 0.006.
Values may be sent and summed in bfloat16 or wider, within the bound.
A program may use at most 32 MiB of HBM per device.

```python
import math
import jax
import jax.numpy as jnp
from jax import lax

CH = 128
NH = 8
HD = 16
COMP = 25
NQ = 16
NK = 2048
KMAX = 7
BS = 256
NNB = 3
NBLK = 1024
ATOMS = 262144


def query_key_pair(key):
    first_key, second_key = jax.random.split(jax.random.fold_in(key, 7), 2)
    query_draw = jnp.clip(jax.random.normal(first_key, (NH, HD, ATOMS), jnp.float32), -6.0, 6.0)
    key_draw = jnp.clip(jax.random.normal(second_key, (NH, HD, ATOMS), jnp.float32), -6.0, 6.0)
    return (query_draw, key_draw)


def draw_queries(key, part):
    return query_key_pair(key)[0].astype(jnp.bfloat16)


def draw_key_states(key, part):
    return query_key_pair(key)[1].astype(jnp.bfloat16)


def draw_neighbors(key, part):
    inner_key = jax.random.fold_in(key, 11)
    block_ids = jnp.arange(NBLK)
    offsets = jnp.arange(5) - 2
    candidates = block_ids[:, None] + offsets[None, :]
    inside = (candidates >= 0) & (candidates < NBLK)
    random_bits = jax.random.randint(inner_key, (NBLK, 5), 0, 1 << 20) * 8 + jnp.arange(5)[None, :]
    ranking = jnp.where(offsets[None, :] == 0, -1, jnp.where(inside, random_bits, (1 << 24) + random_bits))
    order = jnp.argsort(ranking, axis=1)
    chosen = jnp.take_along_axis(candidates, order[:, :NNB], axis=1)
    return chosen.astype(jnp.int32)


def draw_integer_wave_vectors(key, part):
    inner_key = jax.random.fold_in(key, 13)
    numbers = jax.random.randint(inner_key, (3, NK), -KMAX, KMAX + 1)
    all_zero = jnp.all(numbers == 0, axis=0)
    numbers = jnp.where((jnp.arange(3)[:, None] == 0) & all_zero[None, :], 1, numbers)
    return numbers.astype(jnp.int32)


def plant(values, rng, low, top_value):
    longest = values.shape.index(max(values.shape))
    spots = []
    for shift in (0, 1):
        where = [jax.random.randint(jax.random.fold_in(rng, axis), (), 0, length) for axis, length in enumerate(values.shape)]
        where[longest] = (where[longest] + shift) % values.shape[longest]
        spots.append(tuple(where))
    return values.at[spots[0]].set(low).at[spots[1]].set(top_value)


def steps_of(stream_key, extent, shards, smallest, largest):
    loudness, own = 1.0, jax.random.fold_in(stream_key, 6)
    for dim, blocks in shards:
        draws = jnp.exp(jax.random.uniform(jax.random.fold_in(own, dim), (blocks,), jnp.float32, smallest / len(shards), largest / len(shards)))
        loudness = loudness * jnp.repeat(draws, extent[dim] // blocks).reshape([-1 if axis == dim else 1 for axis in range(len(extent))])
    return loudness


def noise(rng, dims, spread, most, cuts=(), dtype=jnp.bfloat16):
    result = jax.random.normal(rng, dims, jnp.float32) * spread
    if len(cuts) > 0:
        result = steps_of(rng, dims, cuts, -0.22, 0.18) * result
    return jnp.clip(result, min=-most, max=most).astype(dtype)


def setup_inputs(seed: int = 0) -> dict:
    splits = jax.random.split(jax.random.key(seed), 9)
    return {
        "queries": draw_queries(jax.random.fold_in(splits[8], 71), 0),
        "key_states": draw_key_states(jax.random.fold_in(splits[8], 71), 0),
        "value_states": noise(splits[2], (CH, COMP, ATOMS), 8.0, 48.0, ((0, 8), (2, 128))),
        "fractional": jnp.clip(1.0 * jax.random.uniform(splits[3], (3, ATOMS), jnp.float32) ** steps_of(splits[3], (3, ATOMS), ((1, 128),), -0.2, 0.2), 0.0, 1.0),
        "block_counts": plant(jax.random.randint(splits[4], (NBLK,), BS // 4, BS + 1), jax.random.fold_in(splits[4], 1), BS // 4, BS).astype(jnp.int32),
        "neighbors": draw_neighbors(jax.random.fold_in(splits[8], 71), 0),
        "integer_wave_vectors": draw_integer_wave_vectors(jax.random.fold_in(splits[8], 71), 0),
        "charge_weight": noise(splits[7], (CH, NQ), CH ** -0.5, 0.5, ((0, 8),)),
    }


ewald_scale = 40.0
ewald_damp = 0.02

def attend_block(query_block, gathered, valid_keys, own_count, head_dim):
    key_part = gathered[:, :head_dim].astype(jnp.float32)
    value_part = gathered[:, head_dim:].astype(jnp.float32)
    scores = jnp.einsum('hdq,hdk->hqk', query_block.astype(jnp.float32), key_part) * head_dim ** (-0.5)
    scores = jnp.where(valid_keys[None, None, :], scores, -jnp.inf)
    row_max = lax.optimization_barrier(jnp.max(scores, axis=2, keepdims=True))
    weights = jnp.exp(scores - row_max)
    denominator = lax.optimization_barrier(jnp.sum(weights, axis=2))
    rounded = weights.astype(jnp.bfloat16).astype(jnp.float32)
    mixture = jnp.einsum('hck,hqk->hcq', value_part, rounded) / denominator[:, None, :]
    live_rows = jnp.arange(query_block.shape[2]) < own_count
    return jnp.where(live_rows[None, None, :], mixture, 0.0).astype(jnp.bfloat16)

def plane_wave_terms(reciprocal_vectors, atom_positions):
    phase_angles = 2.0 * math.pi * (reciprocal_vectors[0][:, None] * atom_positions[0][None, :] + reciprocal_vectors[1][:, None] * atom_positions[1][None, :] + reciprocal_vectors[2][:, None] * atom_positions[2][None, :])
    return (jnp.cos(phase_angles), jnp.sin(phase_angles))

def contract(atom_charges, wave_table):
    return lax.dot_general(atom_charges, wave_table, (((1,), (1,)), ((), ())), precision=lax.Precision.HIGHEST, preferred_element_type=jnp.float32)

def potential_field_values(atom_charges, cosine_phase_values, sine_phase_values, reciprocal_vectors, reciprocal_weight, structure_real, structure_imaginary):
    query_block_count = structure_real.shape[0]
    wave_vector_count = structure_real.shape[1]
    weighted_real_part = structure_real * reciprocal_weight[None, :]
    weighted_imaginary = structure_imaginary * reciprocal_weight[None, :]
    cosine_product = jnp.concatenate([weighted_real_part, -(weighted_imaginary[None] * reciprocal_vectors[:, None, :]).reshape(3 * query_block_count, wave_vector_count)], axis=0)
    sine_product = jnp.concatenate([weighted_imaginary, (weighted_real_part[None] * reciprocal_vectors[:, None, :]).reshape(3 * query_block_count, wave_vector_count)], axis=0)
    combined = jnp.dot(cosine_product, cosine_phase_values, precision=lax.Precision.HIGHEST, preferred_element_type=jnp.float32) + jnp.dot(sine_product, sine_phase_values, precision=lax.Precision.HIGHEST, preferred_element_type=jnp.float32)
    potential = combined[:query_block_count]
    gradient = combined[query_block_count:].reshape(3, query_block_count, -1)
    forces = lax.optimization_barrier(jnp.sum(atom_charges[None] * gradient, axis=1))
    return (potential, forces)

def reference(queries, key_states, value_states, fractional, block_counts, neighbors, integer_wave_vectors, charge_weight):
    head_chan = CH // NH
    row_width = HD + head_chan * COMP
    stacked = jnp.concatenate([key_states, value_states.reshape(NH, head_chan * COMP, ATOMS)], axis=1).reshape(NH, row_width, NBLK, BS)
    slot_ids = jnp.arange(BS)
    valid_all = slot_ids[None, :] < block_counts[:, None]
    query_blocks = queries.reshape(NH, HD, NBLK, BS).transpose(2, 0, 1, 3)

    def one_block(inputs):
        query_block, listed, own_count = inputs
        gathered = jnp.take(stacked, listed, axis=2).reshape(NH, row_width, NNB * BS)
        valid_keys = jnp.take(valid_all, listed, axis=0).reshape(NNB * BS)
        return attend_block(query_block, gathered, valid_keys, own_count, HD)
    blocks_out = lax.map(one_block, (query_blocks, neighbors, block_counts))
    attention = blocks_out.transpose(1, 2, 0, 3).reshape(CH, COMP, ATOMS)
    atom_charges = jnp.dot(charge_weight.T, attention[:, 0, :], preferred_element_type=jnp.float32)
    reciprocal_vectors = integer_wave_vectors.astype(jnp.float32)
    squared_norm = lax.optimization_barrier(jnp.sum(reciprocal_vectors * reciprocal_vectors, axis=0))
    reciprocal_weight = ewald_scale * jnp.exp(-ewald_damp * squared_norm) / squared_norm
    inv_root = 1.0 / math.sqrt(ATOMS)
    charge_blocks = atom_charges.reshape(NQ, NBLK, BS).transpose(1, 0, 2)
    coord_blocks = fractional.reshape(3, NBLK, BS).transpose(1, 0, 2)

    def add_block(running, inputs):
        block_atom_charges, block_atom_positions = inputs
        cosine_phase_values, sine_phase_values = plane_wave_terms(reciprocal_vectors, block_atom_positions)
        return ((running[0] + contract(block_atom_charges, cosine_phase_values) * inv_root, running[1] + contract(block_atom_charges, sine_phase_values) * inv_root), None)
    start = (jnp.zeros((NQ, NK), jnp.float32), jnp.zeros((NQ, NK), jnp.float32))
    (structure_real, structure_imaginary), _ = lax.scan(add_block, start, (charge_blocks, coord_blocks))

    def field_block(inputs):
        block_atom_charges, block_atom_positions = inputs
        cosine_phase_values, sine_phase_values = plane_wave_terms(reciprocal_vectors, block_atom_positions)
        return potential_field_values(block_atom_charges, cosine_phase_values, sine_phase_values, reciprocal_vectors, reciprocal_weight, structure_real, structure_imaginary)
    potential_blocks, force_blocks = lax.map(field_block, (charge_blocks, coord_blocks))
    potential = potential_blocks.transpose(1, 0, 2).reshape(NQ, ATOMS)
    forces = force_blocks.transpose(1, 0, 2).reshape(3, ATOMS)
    return (attention, potential, forces)
```

```python
import jax
import jax.numpy as jnp
from jax import lax
from jax.experimental import pallas as pl
from jax.experimental.pallas import tpu as pltpu
from jax.sharding import Mesh
from jax.sharding import PartitionSpec as P

BS = 256
NNB = 3
NY, NZ, NX, NC = 4, 32, 4, 2
SEQ = ("y", "z")
INNER = ("x", "c")
NI = NX * NC
NSEQ = NY * NZ
GZ = 2
NG = NY * GZ
NR = NZ // GZ
NB = 8
F32, BF16 = jnp.float32, jnp.bfloat16
MESH = pl.DeviceIdType.MESH
DEAD = -1e30

ewald_scale = 40.0
ewald_damp = 0.02

COS = (1.0, -19.739208221435547, 64.93939208984375, -85.45665740966797, 60.242130279541016, -26.4046688079834, 7.800131320953369, -1.4531123638153076)
SIN = (6.2831854820251465, -41.34170150756836, 81.6052474975586, -76.70575714111328, 42.057369232177734, -15.084554672241211, 3.7759575843811035, -0.6150599718093872)


def poly(coeffs, u):
    y = jnp.full_like(u, coeffs[-1])
    for k in coeffs[-2::-1]:
        y = y * u + k
    return y


def cos_sin_turns(t):
    r = t - jnp.floor(t + 0.5)
    u = r * r
    return poly(COS, u), poly(SIN, u) * r


def nt(a, b):
    return lax.dot_general(a, b, (((1,), (1,)), ((), ())), preferred_element_type=F32)


def tn(a, b):
    return lax.dot_general(a, b, (((0,), (0,)), ((), ())), preferred_element_type=F32)


def nn(a, b):
    return jnp.dot(a, b, preferred_element_type=F32)


def kernel(
    q, k, frac, counts, nbr, iwv, cw, v_hbm,
    o_att, o_pot, o_for,
    v_own, v2, ks, qs, ps, rden, ob, v0f, a0, cwa, chg, xt, bt, wt, gs, rs, os_, gt, hs,
    sem_v, sem_o, halo_s, halo_r, a_s, a_r, c_s, c_r, r_s, r_r, f_s, f_r, t_s, t_r, g_s, g_r,
):
    y, z, x, c = (lax.axis_index(a) for a in ("y", "z", "x", "c"))
    inner = x * NC + c
    seq = y * NZ + z
    gid = y * GZ + lax.rem(z, GZ)
    rid = z // GZ
    first = seq * NB

    def at_seq(s):
        return {"y": s // NZ, "z": lax.rem(s, NZ)}

    def listed_at(g, j):
        return jnp.clip(nbr[g, j] - (first - 2), 0, NB + 3)

    right = at_seq(lax.rem(seq + 1, NSEQ))
    left = at_seq(lax.rem(seq + NSEQ - 1, NSEQ))

    def inner_peer(o):
        p = lax.rem(inner + o, NI)
        return p, {"x": p // NC, "c": lax.rem(p, NC)}

    def group_peer(o):
        p = lax.rem(gid + o, NG)
        return p, {"y": p // GZ, "z": rid * GZ + lax.rem(p, GZ)}

    def ring_peer(o):
        p = lax.rem(rid + o, NR)
        return p, {"z": p * GZ + lax.rem(z, GZ)}

    barrier = pltpu.get_barrier_semaphore()
    peers = [left, right]
    peers += [inner_peer(o)[1] for o in range(1, NI)]
    peers += [group_peer(o)[1] for o in range(1, NG)]
    peers += [ring_peer(o)[1] for o in range(1, NR)]
    for p in peers:
        pl.semaphore_signal(barrier, inc=1, device_id=p, device_id_type=MESH)

    load_v = pltpu.make_async_copy(v_hbm, v_own, sem_v)
    load_v.start()

    row16 = lax.broadcasted_iota(jnp.int32, (16, BS), 0)
    lane16 = lax.broadcasted_iota(jnp.int32, (16, BS), 1)
    for b in range(NB):
        cols = pl.ds(b * BS, BS)
        live = lane16 < counts[first + b]
        bias = jnp.where((row16 == 0) & jnp.logical_not(live), DEAD, 0.0)
        ks[b + 2, 0:16, :] = k[0, :, cols]
        ks[b + 2, 16:32, :] = bias.astype(BF16)
        qs[b, 0:16, :] = (q[0, :, cols].astype(F32) * 0.25).astype(BF16)
        qs[b, 16:32, :] = jnp.where(row16 == 0, 1.0, 0.0).astype(BF16)
    cwa[inner] = cw[...]

    load_v.wait()
    for ch in range(16):
        v0f[ch : ch + 1, :] = v_own[ch, 0:1, :].astype(F32)
    for b in range(NB):
        ks[b + 2, 32:48, :] = v0f[:, b * BS : (b + 1) * BS].astype(BF16)

    def send(src, dst, ssem, rsem, dev):
        cp = pltpu.make_async_remote_copy(
            src_ref=src, dst_ref=dst, send_sem=ssem, recv_sem=rsem, device_id=dev, device_id_type=MESH
        )
        cp.start()
        return cp

    pl.semaphore_wait(barrier, len(peers))
    kh = [
        send(ks.at[pl.ds(8, 2)], ks.at[pl.ds(0, 2)], halo_s.at[0], halo_r.at[0], right),
        send(ks.at[pl.ds(2, 2)], ks.at[pl.ds(10, 2)], halo_s.at[1], halo_r.at[1], left),
    ]
    cws = [
        send(cwa.at[inner], cwa.at[inner], c_s.at[o - 1], c_r.at[o - 1], inner_peer(o)[1])
        for o in range(1, NI)
    ]

    @pl.loop(0, NB)
    def _(b):
        for ch in range(16):
            v2[b + 2, ch, 0:25, :] = v_own[ch, :, pl.ds(pl.multiple_of(b * BS, BS), BS)]

    vh = [
        send(v2.at[pl.ds(8, 2)], v2.at[pl.ds(0, 2)], halo_s.at[2], halo_r.at[2], right),
        send(v2.at[pl.ds(2, 2)], v2.at[pl.ds(10, 2)], halo_s.at[3], halo_r.at[3], left),
    ]
    for cp in kh:
        cp.wait_recv()

    @pl.loop(0, NB)
    def _(g):
        listed = [listed_at(g, j) for j in range(NNB)]
        qa = qs[g]
        s = [tn(ks[i, 0:32, :], qa) for i in listed]
        m = s[0].max(axis=0, keepdims=True)
        for t in s[1:]:
            m = jnp.maximum(m, t.max(axis=0, keepdims=True))
        den = jnp.zeros((1, BS), F32)
        acc = jnp.zeros((16, BS), F32)
        for j, i in enumerate(listed):
            w = jnp.exp(s[j] - m)
            den += w.sum(axis=0, keepdims=True)
            wb = w.astype(BF16)
            ps[g, j] = wb
            acc += nn(ks[i, 32:48, :], wb)
        live_q = lax.broadcasted_iota(jnp.int32, (1, BS), 1) < counts[first + g]
        rd = jnp.where(live_q, 1.0 / den, 0.0)
        rden[g] = rd
        a0[inner, :, pl.ds(pl.multiple_of(g * BS, BS), BS)] = (acc * rd).astype(BF16)

    asend = [
        send(a0.at[inner], a0.at[inner], a_s.at[o - 1], a_r.at[o - 1], inner_peer(o)[1])
        for o in range(1, NI)
    ]

    n_atoms = NB * BS
    iota8 = lax.broadcasted_iota(jnp.int32, (8, n_atoms), 0).astype(F32)
    xc, xs = cos_sin_turns(frac[0:1, :] * iota8)
    xt[0] = xc
    xt[1] = xs
    u_tab = cos_sin_turns(frac[1:2, :] * iota8)
    v_tab = cos_sin_turns(frac[2:3, :] * iota8)
    for u in range(2):
        for v in range(2):
            for n in range(0, 8, 2):
                lo = u_tab[u][n : n + 1, :] * v_tab[v]
                hi = u_tab[u][n + 1 : n + 2, :] * v_tab[v]
                at = u * 128 + v * 64 + n * 8
                bt[at : at + 16, :] = jnp.concatenate([lo, hi], axis=0).astype(BF16)

    n0, n1, n2 = iwv[0:1, :], iwv[1:2, :], iwv[2:3, :]
    n_waves = iwv.shape[1]
    flip = n0 < 0
    n1 = jnp.where(flip, -n1, n1)
    n2 = jnp.where(flip, -n2, n2)
    s1 = jnp.where(n1 < 0, -1.0, 1.0)
    s2 = jnp.where(n2 < 0, -1.0, 1.0)
    place = jnp.abs(n1) * 8 + jnp.abs(n2)
    rows128 = lax.broadcasted_iota(jnp.int32, (128, n_waves), 0)
    hot = jnp.where((rows128 & 63) == place, 1.0, 0.0).astype(BF16)
    mine = lax.broadcasted_iota(jnp.int32, (8, n_waves), 0) == jnp.abs(n0)
    coeffs = [jnp.ones_like(s1), s1, s2, s1 * s2]
    listed = jnp.concatenate([jnp.where(mine, cf, 0.0) for cf in coeffs], axis=0).astype(BF16)
    cnt = nt(listed, hot)
    d_row = lax.broadcasted_iota(jnp.int32, (8, 128), 0)
    l_row = lax.broadcasted_iota(jnp.int32, (8, 128), 1)
    b_row = (l_row & 63) >> 3
    g_row = l_row & 7
    norm2 = jnp.maximum(d_row * d_row + b_row * b_row + g_row * g_row, 1).astype(F32)
    kw = ewald_scale * jnp.exp(-ewald_damp * norm2) / norm2
    for t in range(4):
        wt[t] = cnt[t * 8 : (t + 1) * 8] * kw

    for cp in cws + asend:
        cp.wait_recv()
    charges = tn(cwa[...].reshape(NI * 16, 16), a0[...].reshape(NI * 16, n_atoms))
    chg[...] = charges

    own_c = xt[0, pl.ds(inner, 1), :]
    own_s = xt[1, pl.ds(inner, 1), :]
    amp = jnp.concatenate([charges * own_c, charges * own_s], axis=0) * (1.0 / 512.0)
    amp_h = amp.astype(BF16)
    amp_l = (amp - amp_h.astype(F32)).astype(BF16)
    both = nt(jnp.concatenate([amp_h, amp_l], axis=0), bt[...])
    part = both[0:32] + both[32:64]
    for p in range(8):
        gs[p] = part[(p // 2) * 8 : (p // 2) * 8 + 8, (p % 2) * 128 : (p % 2) * 128 + 128]

    rsend = []
    for o in range(1, NG):
        p, dev = group_peer(o)
        rsend.append(send(gs.at[p], rs.at[gid], r_s.at[o - 1], r_r.at[o - 1], dev))
    rs[gid] = gs[gid]
    for cp in rsend:
        cp.wait_recv()
    os_[rid] = jnp.sum(rs[...], axis=0)
    fsend = [
        send(os_.at[rid], os_.at[rid], f_s.at[o - 1], f_r.at[o - 1], ring_peer(o)[1])
        for o in range(1, NR)
    ]

    for cp in vh:
        cp.wait_recv()

    @pl.loop(0, NB)
    def _(g):
        acc = jnp.zeros((512, BS), F32)
        for j in range(NNB):
            i = listed_at(g, j)
            acc += nn(v2[i].reshape(512, BS), ps[g, j])
        ob[g] = (acc * rden[g]).astype(BF16).reshape(16, 32, BS)

    outs = []
    for g in range(NB):
        cp = pltpu.make_async_copy(ob.at[g], o_att.at[:, :, pl.ds(g * BS, BS)], sem_o.at[g])
        cp.start()
        outs.append(cp)

    for cp in fsend:
        cp.wait_recv()
    gt[inner, gid] = jnp.sum(os_[...], axis=0)
    tsend = [
        send(gt.at[inner, gid], gt.at[inner, gid], t_s.at[o - 1], t_r.at[o - 1], group_peer(o)[1])
        for o in range(1, NG)
    ]
    for cp in tsend:
        cp.wait_recv()
    gsend = [
        send(gt.at[inner], gt.at[inner], g_s.at[o - 1], g_r.at[o - 1], inner_peer(o)[1])
        for o in range(1, NI)
    ]
    for cp in gsend:
        cp.wait_recv()

    lane = lax.broadcasted_iota(jnp.int32, (1, 128), 1)
    sgn = jnp.where(lane < 64, -1.0, 1.0)
    w_n1 = ((lane & 63) >> 3).astype(F32)
    w_n2 = (lane & 7).astype(F32)

    def swap(a):
        return pltpu.roll(a, 64, 1)

    for d in range(NI):
        w0, w1, w2, w12 = (wt[t, d : d + 1, :] for t in range(4))
        g4 = {
            (p, u): jnp.concatenate([gt[d, 4 * p + u], gt[d, 4 * p + 2 + u]], axis=0)
            for p in range(2)
            for u in range(2)
        }
        h = {}
        for p in range(2):
            for u in range(2):
                su = sgn if u == 0 else -sgn
                sp = sgn if p == 0 else -sgn
                pu = -1.0 if p == u else 1.0
                h[p, u] = (
                    w0 * g4[p, u]
                    + (su * w12) * swap(g4[p, 1 - u])
                    + (pu * w1) * g4[1 - p, 1 - u]
                    + (sp * w2) * swap(g4[1 - p, u])
                )
        for p in range(2):
            r = p * 16
            hs[d, r : r + 16, 0:128] = h[p, 0].astype(BF16)
            hs[d, r : r + 16, 128:256] = h[p, 1].astype(BF16)
            hs[d, 32 + r : 48 + r, 0:128] = (-w_n1 * h[p, 1]).astype(BF16)
            hs[d, 32 + r : 48 + r, 128:256] = (w_n1 * h[p, 0]).astype(BF16)
            for u in range(2):
                hs[d, 64 + r : 80 + r, u * 128 : u * 128 + 128] = (
                    (w_n2 * sgn) * swap(h[p, u])
                ).astype(BF16)

    @pl.loop(0, NB)
    def _(t):
        cols = pl.ds(pl.multiple_of(t * BS, BS), BS)
        basis = bt[:, cols]
        pot = jnp.zeros((16, BS), F32)
        fx = jnp.zeros((16, BS), F32)
        fy = jnp.zeros((16, BS), F32)
        fz = jnp.zeros((16, BS), F32)
        for d in range(NI):
            r = nn(hs[d], basis)
            xc = xt[0, d : d + 1, cols]
            xs = xt[1, d : d + 1, cols]
            pot += xc * r[0:16] + xs * r[16:32]
            if d:
                fx += (d * xs) * r[0:16] - (d * xc) * r[16:32]
            fy += xc * r[32:48] + xs * r[48:64]
            fz += xc * r[64:80] + xs * r[80:96]
        o_pot[:, cols] = pot
        ch = chg[:, cols]
        for i, f in enumerate((fx, fy, fz)):
            o_for[i : i + 1, cols] = jnp.sum(ch * f, axis=0, keepdims=True)

    for cp in outs:
        cp.wait()
    for cp in kh + cws + vh + asend + rsend + fsend + tsend + gsend:
        cp.wait_send()


def local(queries, key_states, value_states, fractional, block_counts, neighbors, integer_wave_vectors, charge_weight):
    n_atoms = queries.shape[2]
    vmem = pl.BlockSpec(memory_space=pltpu.VMEM)
    smem = pl.BlockSpec(memory_space=pltpu.SMEM)
    hbm = pl.BlockSpec(memory_space=pl.ANY)
    dma = pltpu.SemaphoreType.DMA
    attention, potential, forces = pl.pallas_call(
        kernel,
        out_shape=(
            jax.ShapeDtypeStruct((16, 32, n_atoms), BF16),
            jax.ShapeDtypeStruct((16, n_atoms), F32),
            jax.ShapeDtypeStruct((3, n_atoms), F32),
        ),
        in_specs=[vmem, vmem, vmem, smem, smem, vmem, vmem, hbm],
        out_specs=(hbm, vmem, vmem),
        scratch_shapes=[
            pltpu.VMEM((16, 25, n_atoms), BF16),
            pltpu.VMEM((NB + 4, 16, 32, BS), BF16),
            pltpu.VMEM((NB + 4, 48, BS), BF16),
            pltpu.VMEM((NB, 32, BS), BF16),
            pltpu.VMEM((NB, NNB, BS, BS), BF16),
            pltpu.VMEM((NB, 1, BS), F32),
            pltpu.VMEM((NB, 16, 32, BS), BF16),
            pltpu.VMEM((16, n_atoms), F32),
            pltpu.VMEM((NI, 16, n_atoms), BF16),
            pltpu.VMEM((NI, 16, 16), BF16),
            pltpu.VMEM((16, n_atoms), F32),
            pltpu.VMEM((2, 8, n_atoms), F32),
            pltpu.VMEM((256, n_atoms), BF16),
            pltpu.VMEM((4, 8, 128), F32),
            pltpu.VMEM((NG, 8, 128), F32),
            pltpu.VMEM((NG, 8, 128), F32),
            pltpu.VMEM((NR, 8, 128), F32),
            pltpu.VMEM((NI, NG, 8, 128), F32),
            pltpu.VMEM((NI, 96, 256), BF16),
            dma,
            dma((NB,)),
            dma((4,)),
            dma((4,)),
            dma((NI - 1,)),
            dma((NI - 1,)),
            dma((NI - 1,)),
            dma((NI - 1,)),
            dma((NG - 1,)),
            dma((NG - 1,)),
            dma((NR - 1,)),
            dma((NR - 1,)),
            dma((NG - 1,)),
            dma((NG - 1,)),
            dma((NI - 1,)),
            dma((NI - 1,)),
        ],
        compiler_params=pltpu.CompilerParams(
            collective_id=0, has_side_effects=True, vmem_limit_bytes=40 << 20
        ),
    )(queries, key_states, fractional, block_counts, neighbors, integer_wave_vectors, charge_weight, value_states)
    return attention[:, :25, :], potential, forces


def solution(mesh):
    torus = Mesh(mesh.devices.reshape(NY, NZ, NX, NC), ("y", "z", "x", "c"))
    return jax.shard_map(
        local,
        mesh=torus,
        in_specs=(
            P(INNER, None, SEQ),
            P(INNER, None, SEQ),
            P(INNER, None, SEQ),
            P(None, SEQ),
            P(),
            P(SEQ, None),
            P(),
            P(INNER, None),
        ),
        out_specs=(P(INNER, None, SEQ), P(None, SEQ), P(None, SEQ)),
        check_vma=False,
    )
```

```python
import jax
import jax.numpy as jnp
from jax import lax
from jax.experimental import pallas as pl
from jax.experimental.pallas import tpu as pltpu
from jax.sharding import Mesh
from jax.sharding import PartitionSpec as P

BS = 256
NNB = 3
NY, NZ, NX, NC = 4, 32, 4, 2
SEQ = ("y", "z")
INNER = ("x", "c")
NI = NX * NC
NSEQ = NY * NZ
GZ = 2
NG = NY * GZ
NR = NZ // GZ
NB = 8
F32, BF16 = jnp.float32, jnp.bfloat16
MESH = pl.DeviceIdType.MESH
DEAD = -1e30

ewald_scale = 40.0
ewald_damp = 0.02

COS = (1.0, -19.739208221435547, 64.93939208984375, -85.45665740966797, 60.242130279541016, -26.4046688079834, 7.800131320953369, -1.4531123638153076)
SIN = (6.2831854820251465, -41.34170150756836, 81.6052474975586, -76.70575714111328, 42.057369232177734, -15.084554672241211, 3.7759575843811035, -0.6150599718093872)


def poly(coeffs, u):
    y = jnp.full_like(u, coeffs[-1])
    for k in coeffs[-2::-1]:
        y = y * u + k
    return y


def cos_sin_turns(t):
    r = t - jnp.floor(t + 0.5)
    u = r * r
    return poly(COS, u), poly(SIN, u) * r


def nt(a, b):
    return lax.dot_general(a, b, (((1,), (1,)), ((), ())), preferred_element_type=F32)


def tn(a, b):
    return lax.dot_general(a, b, (((0,), (0,)), ((), ())), preferred_element_type=F32)


def nn(a, b):
    return jnp.dot(a, b, preferred_element_type=F32)


def listed_at(nbr, g, j, low, high):
    return jnp.clip(nbr[j, g] - low, 0, high)


def kernel(
    q_hbm, k_hbm, frac_hbm, counts_hbm, nbr_hbm, iwv_hbm, cw_hbm, v_hbm,
    att_hbm, gt_hbm, wt_hbm, xt_hbm, bt_hbm, chg_hbm,
    ob, gt, wt, xt, bt, chg, sem_o,
    q, k, frac, counts, nbr, iwv, cw, sem_i, v2, v0, ks, kin, kb, qs, ps, rden, a0, cwa, gs, rs, os_,
    sem_v, sem_v0, known, halo_s, halo_r, a_s, a_r, af_s, af_r, c_s, c_r, r_s, r_r, f_s, f_r, t_s, t_r, g_s, g_r, gf_s, gf_r,
):
    y, z, x, c = (lax.axis_index(a) for a in ("y", "z", "x", "c"))
    inner = x * NC + c
    seq = y * NZ + z
    gid = y * GZ + lax.rem(z, GZ)
    rid = z // GZ
    first = seq * NB

    def at_seq(s):
        return {"y": s // NZ, "z": lax.rem(s, NZ)}

    right = at_seq(lax.rem(seq + 1, NSEQ))
    left = at_seq(lax.rem(seq + NSEQ - 1, NSEQ))
    other = {"c": 1 - c}

    def inner_peer(o):
        p = lax.rem(inner + o, NI)
        return {"x": p // NC, "c": lax.rem(p, NC)}

    def x_peer(o):
        return {"x": lax.rem(x + o, NX)}

    def x_from(o):
        return lax.rem(x + NX - o, NX) * NC + c

    def group_peer(o):
        p = lax.rem(gid + o, NG)
        return p, {"y": p // GZ, "z": rid * GZ + lax.rem(p, GZ)}

    def ring_peer(o):
        p = lax.rem(rid + o, NR)
        return {"z": p * GZ + lax.rem(z, GZ)}

    pairs = ((k_hbm, k), (counts_hbm, counts), (q_hbm, q), (cw_hbm, cw), (nbr_hbm, nbr), (frac_hbm, frac), (iwv_hbm, iwv))
    takes = [pltpu.make_async_copy(a, b, sem_i.at[i]) for i, (a, b) in enumerate(pairs)]
    load_v0 = pltpu.make_async_copy(v_hbm.at[0], v0, sem_v0)
    for cp in takes[:2] + [load_v0] + takes[2:]:
        cp.start()

    barrier = pltpu.get_barrier_semaphore()
    near = [left, right, ring_peer(1), ring_peer(NR - 1)]
    near += [inner_peer(o) for o in range(1, NI)]
    near += [group_peer(o)[1] for o in range(1, NG)]
    for p in near:
        pl.semaphore_signal(barrier, inc=1, device_id=p, device_id_type=MESH)

    def tell(r):
        for o in (1 << r, NR - (1 << r)):
            pl.semaphore_signal(known.at[r], inc=1, device_id=ring_peer(o), device_id_type=MESH)

    def hear(r):
        pl.semaphore_wait(known.at[r], 2)

    loads = []
    for b in (0, 1, 6, 7, 2, 3, 4, 5):
        cp = pltpu.make_async_copy(v_hbm.at[:, :, pl.ds(b * BS, BS)], v2.at[b + 2], sem_v.at[b])
        cp.start()
        loads.append(cp)

    for cp in takes[:5]:
        cp.wait()

    row16 = lax.broadcasted_iota(jnp.int32, (16, BS), 0)
    lane16 = lax.broadcasted_iota(jnp.int32, (16, BS), 1)
    for b in range(NB):
        cols = pl.ds(b * BS, BS)
        live = lane16 < counts[first + b]
        bias = jnp.where((row16 == 0) & jnp.logical_not(live), DEAD, 0.0)
        ks[b, 0:16, :] = k[0, :, cols]
        ks[b, 16:32, :] = bias.astype(BF16)
        qs[b, 0:16, :] = (q[0, :, cols].astype(F32) * 0.25).astype(BF16)
        qs[b, 16:32, :] = jnp.where(row16 == 0, 1.0, 0.0).astype(BF16)
    cwa[inner] = cw[...]
    load_v0.wait()
    for b in range(NB):
        ks[b, 32:48, :] = v0[:, b * BS : (b + 1) * BS]

    def send(src, dst, ssem, rsem, dev):
        cp = pltpu.make_async_remote_copy(
            src_ref=src, dst_ref=dst, send_sem=ssem, recv_sem=rsem, device_id=dev, device_id_type=MESH
        )
        cp.start()
        return cp

    pl.semaphore_wait(barrier, len(near))
    kh = [
        send(ks.at[pl.ds(6, 2)], kin.at[pl.ds(0, 2)], halo_s.at[0], halo_r.at[0], right),
        send(ks.at[pl.ds(0, 2)], kin.at[pl.ds(2, 2)], halo_s.at[1], halo_r.at[1], left),
    ]
    tell(0)
    cws = [
        send(cwa.at[inner], cwa.at[inner], c_s.at[o - 1], c_r.at[o - 1], inner_peer(o))
        for o in range(1, NI)
    ]
    for cp in loads[:4]:
        cp.wait()
    vh = [
        send(v2.at[pl.ds(8, 2)], v2.at[pl.ds(0, 2)], halo_s.at[2], halo_r.at[2], right),
        send(v2.at[pl.ds(2, 2)], v2.at[pl.ds(10, 2)], halo_s.at[3], halo_r.at[3], left),
    ]

    def attend(src, low, high, at):
        g = lax.rem(at + 2, NB)
        listed = [listed_at(nbr, g, j, low, high) for j in range(NNB)]
        qa = qs[g]
        s = [tn(src[i, 0:32, :], qa) for i in listed]
        m = s[0].max(axis=0, keepdims=True)
        for t in s[1:]:
            m = jnp.maximum(m, t.max(axis=0, keepdims=True))
        den = jnp.zeros((1, BS), F32)
        acc = jnp.zeros((16, BS), F32)
        for j, i in enumerate(listed):
            w = jnp.exp(s[j] - m)
            den += w.sum(axis=0, keepdims=True)
            wb = w.astype(BF16)
            ps[g, j] = wb
            acc += nn(src[i, 32:48, :], wb)
        live_q = lax.broadcasted_iota(jnp.int32, (1, BS), 1) < counts[first + g]
        rd = jnp.where(live_q, 1.0 / den, 0.0)
        rden[g] = rd
        a0[inner, at] = (acc * rd).astype(BF16)

    def spread(half):
        mine = a0.at[inner, pl.ds(4 * half, 4)]
        out = [send(mine, mine, a_s.at[half, o - 1], a_r.at[half, o - 1], x_peer(o)) for o in range(1, NX)]
        return out, [send(mine, mine, af_s.at[half, 0], af_r.at[half, 0], other)]

    def pass_on(half, out, on):
        for o in range(1, NX):
            out[o - 1].wait_recv()
            got = a0.at[x_from(o), pl.ds(4 * half, 4)]
            on.append(send(got, got, af_s.at[half, o], af_r.at[half, o], other))

    @pl.loop(0, 4)
    def _(at):
        attend(ks, first, NB - 1, at)

    out0, on0 = spread(0)
    for cp in kh:
        cp.wait_recv()
    hear(0)
    tell(1)
    kb[0:2] = kin[0:2]
    kb[2:10] = ks[...]
    kb[10:12] = kin[2:4]

    @pl.loop(4, 8)
    def _(at):
        attend(kb, first - 2, NB + 3, at)

    out1, on1 = spread(1)
    pass_on(0, out0, on0)
    hear(1)
    tell(2)

    for cp in takes[5:]:
        cp.wait()

    n_atoms = NB * BS
    iota8 = lax.broadcasted_iota(jnp.int32, (8, n_atoms), 0).astype(F32)
    xc, xs = cos_sin_turns(frac[0:1, :] * iota8)
    xt[0] = xc
    xt[1] = xs
    u_tab = cos_sin_turns(frac[1:2, :] * iota8)
    v_tab = cos_sin_turns(frac[2:3, :] * iota8)
    for u in range(2):
        for v in range(2):
            for n in range(0, 8, 2):
                lo = u_tab[u][n : n + 1, :] * v_tab[v]
                hi = u_tab[u][n + 1 : n + 2, :] * v_tab[v]
                at = u * 128 + v * 64 + n * 8
                bt[at : at + 16, :] = jnp.concatenate([lo, hi], axis=0).astype(BF16)

    stored = []

    def store(i, src, dst):
        cp = pltpu.make_async_copy(src, dst, sem_o.at[i])
        cp.start()
        stored.append(cp)

    store(0, bt, bt_hbm)
    store(1, xt, xt_hbm)

    pass_on(1, out1, on1)
    for cp in cws + on0:
        cp.wait_recv()

    def charge(at):
        g = (at + 2) % NB
        r = tn(cwa[...].reshape(NI * 16, 16), a0[:, at].reshape(NI * 16, BS))
        chg[:, g * BS : (g + 1) * BS] = r

    for at in range(4):
        charge(at)
    for cp in on1:
        cp.wait_recv()
    for at in range(4, 8):
        charge(at)

    store(2, chg, chg_hbm)

    charges = chg[...]
    own_c = xt[0, pl.ds(inner, 1), :]
    own_s = xt[1, pl.ds(inner, 1), :]
    amp = jnp.concatenate([charges * own_c, charges * own_s], axis=0) * (1.0 / 512.0)
    amp_h = amp.astype(BF16)
    amp_l = (amp - amp_h.astype(F32)).astype(BF16)
    both = nt(jnp.concatenate([amp_h, amp_l], axis=0), bt[...])
    part = both[0:32] + both[32:64]
    for p in range(8):
        gs[p] = part[(p // 2) * 8 : (p // 2) * 8 + 8, (p % 2) * 128 : (p % 2) * 128 + 128]

    rsend = []
    for o in range(1, NG):
        p, dev = group_peer(o)
        rsend.append(send(gs.at[p], rs.at[gid], r_s.at[o - 1], r_r.at[o - 1], dev))
    rs[gid] = gs[gid]
    hear(2)
    for cp in rsend:
        cp.wait_recv()
    os_[rid] = jnp.sum(rs[...], axis=0)
    fsend = [
        send(os_.at[rid], os_.at[rid], f_s.at[o - 1], f_r.at[o - 1], ring_peer(o))
        for o in range(1, NR)
    ]

    n0, n1, n2 = iwv[0:1, :], iwv[1:2, :], iwv[2:3, :]
    n_waves = iwv.shape[1]
    flip = n0 < 0
    n1 = jnp.where(flip, -n1, n1)
    n2 = jnp.where(flip, -n2, n2)
    s1 = jnp.where(n1 < 0, -1.0, 1.0)
    s2 = jnp.where(n2 < 0, -1.0, 1.0)
    place = jnp.abs(n1) * 8 + jnp.abs(n2)
    rows128 = lax.broadcasted_iota(jnp.int32, (128, n_waves), 0)
    hot = jnp.where((rows128 & 63) == place, 1.0, 0.0).astype(BF16)
    mine = lax.broadcasted_iota(jnp.int32, (8, n_waves), 0) == jnp.abs(n0)
    coeffs = [jnp.ones_like(s1), s1, s2, s1 * s2]
    listed = jnp.concatenate([jnp.where(mine, cf, 0.0) for cf in coeffs], axis=0).astype(BF16)
    cnt = nt(listed, hot)
    d_row = lax.broadcasted_iota(jnp.int32, (8, 128), 0)
    l_row = lax.broadcasted_iota(jnp.int32, (8, 128), 1)
    b_row = (l_row & 63) >> 3
    g_row = l_row & 7
    norm2 = jnp.maximum(d_row * d_row + b_row * b_row + g_row * g_row, 1).astype(F32)
    kw = ewald_scale * jnp.exp(-ewald_damp * norm2) / norm2
    for t in range(4):
        wt[t] = cnt[t * 8 : (t + 1) * 8] * kw
    store(3, wt, wt_hbm)

    for cp in loads[4:]:
        cp.wait()
    for cp in vh:
        cp.wait_recv()

    @pl.loop(0, NB)
    def _(g):
        acc = jnp.zeros((400, BS), F32)
        for j in range(NNB):
            i = listed_at(nbr, g, j, first - 2, NB + 3)
            acc += nn(v2[i].reshape(400, BS), ps[g, j])
        ob[:, :, pl.ds(pl.multiple_of(g * BS, BS), BS)] = (acc * rden[g]).astype(BF16).reshape(25, 16, BS)

    store(4, ob, att_hbm)

    for cp in fsend:
        cp.wait_recv()
    gt[inner, gid] = jnp.sum(os_[...], axis=0)
    tsend = [
        send(gt.at[inner, gid], gt.at[inner, gid], t_s.at[o - 1], t_r.at[o - 1], group_peer(o)[1])
        for o in range(1, NG)
    ]
    for cp in tsend:
        cp.wait_recv()
    gsend = [send(gt.at[inner], gt.at[inner], g_s.at[o - 1], g_r.at[o - 1], x_peer(o)) for o in range(1, NX)]
    gon = [send(gt.at[inner], gt.at[inner], gf_s.at[0], gf_r.at[0], other)]
    for o in range(1, NX):
        gsend[o - 1].wait_recv()
        got = gt.at[x_from(o)]
        gon.append(send(got, got, gf_s.at[o], gf_r.at[o], other))
    for cp in gon:
        cp.wait_recv()
    store(5, gt, gt_hbm)
    for cp in kh + cws + vh + out0 + on0 + out1 + on1 + rsend + fsend + tsend + gsend + gon:
        cp.wait_send()
    for cp in stored:
        cp.wait()


def field(
    att_hbm, gt_hbm, wt_hbm, xt_hbm, bt_hbm, chg_hbm, o_att, o_pot, o_for, att, gt, wt, xt, bt, chg, hs, sem
):
    pairs = ((gt_hbm, gt), (wt_hbm, wt), (bt_hbm, bt), (xt_hbm, xt), (chg_hbm, chg), (att_hbm, att))
    takes = [pltpu.make_async_copy(a, b, sem.at[i]) for i, (a, b) in enumerate(pairs)]
    for cp in takes:
        cp.start()
    for cp in takes[:2]:
        cp.wait()

    lane = lax.broadcasted_iota(jnp.int32, (1, 128), 1)
    sgn = jnp.where(lane < 64, -1.0, 1.0)
    w_n1 = ((lane & 63) >> 3).astype(F32)
    w_n2 = (lane & 7).astype(F32)

    def swap(a):
        return pltpu.roll(a, 64, 1)

    for d in range(NI):
        w0, w1, w2, w12 = (wt[t, d : d + 1, :] for t in range(4))
        g4 = {
            (p, u): jnp.concatenate([gt[d, 4 * p + u], gt[d, 4 * p + 2 + u]], axis=0)
            for p in range(2)
            for u in range(2)
        }
        h = {}
        for p in range(2):
            for u in range(2):
                su = sgn if u == 0 else -sgn
                sp = sgn if p == 0 else -sgn
                pu = -1.0 if p == u else 1.0
                h[p, u] = (
                    w0 * g4[p, u]
                    + (su * w12) * swap(g4[p, 1 - u])
                    + (pu * w1) * g4[1 - p, 1 - u]
                    + (sp * w2) * swap(g4[1 - p, u])
                )
        for p in range(2):
            r = p * 16
            hs[d, r : r + 16, 0:128] = h[p, 0].astype(BF16)
            hs[d, r : r + 16, 128:256] = h[p, 1].astype(BF16)
            hs[d, 32 + r : 48 + r, 0:128] = (-w_n1 * h[p, 1]).astype(BF16)
            hs[d, 32 + r : 48 + r, 128:256] = (w_n1 * h[p, 0]).astype(BF16)
            for u in range(2):
                hs[d, 64 + r : 80 + r, u * 128 : u * 128 + 128] = (
                    (w_n2 * sgn) * swap(h[p, u])
                ).astype(BF16)

    for cp in takes[2:]:
        cp.wait()
    give = pltpu.make_async_copy(att, o_att, sem.at[6])
    give.start()

    @pl.loop(0, NB)
    def _(t):
        cols = pl.ds(pl.multiple_of(t * BS, BS), BS)
        basis = bt[:, cols]
        pot = jnp.zeros((16, BS), F32)
        fx = jnp.zeros((16, BS), F32)
        fy = jnp.zeros((16, BS), F32)
        fz = jnp.zeros((16, BS), F32)
        for d in range(NI):
            r = nn(hs[d], basis)
            xc = xt[0, d : d + 1, cols]
            xs = xt[1, d : d + 1, cols]
            pot += xc * r[0:16] + xs * r[16:32]
            if d:
                fx += (d * xs) * r[0:16] - (d * xc) * r[16:32]
            fy += xc * r[32:48] + xs * r[48:64]
            fz += xc * r[64:80] + xs * r[80:96]
        o_pot[:, cols] = pot
        ch = chg[:, cols]
        for i, f in enumerate((fx, fy, fz)):
            o_for[i : i + 1, cols] = jnp.sum(ch * f, axis=0, keepdims=True)

    give.wait()


def local(queries, key_states, value_states, fractional, block_counts, neighbors, integer_wave_vectors, charge_weight):
    n_atoms = queries.shape[2]
    vmem = pl.BlockSpec(memory_space=pltpu.VMEM)
    hbm = pl.BlockSpec(memory_space=pltpu.HBM)
    dma = pltpu.SemaphoreType.DMA
    att_shape = jax.ShapeDtypeStruct((25, 16, n_atoms), BF16)
    passed = (
        jax.ShapeDtypeStruct((NI, NG, 8, 128), F32),
        jax.ShapeDtypeStruct((4, 8, 128), F32),
        jax.ShapeDtypeStruct((2, 8, n_atoms), F32),
        jax.ShapeDtypeStruct((256, n_atoms), BF16),
        jax.ShapeDtypeStruct((16, n_atoms), F32),
    )
    slots = [pltpu.VMEM(t.shape, t.dtype) for t in passed]
    made = pl.pallas_call(
        kernel,
        out_shape=(att_shape,) + passed,
        in_specs=[hbm] * 8,
        out_specs=(hbm,) * 6,
        scratch_shapes=[pltpu.VMEM(att_shape.shape, BF16)]
        + slots
        + [
            dma((6,)),
            pltpu.VMEM((1, 16, n_atoms), BF16),
            pltpu.VMEM((1, 16, n_atoms), BF16),
            pltpu.VMEM((3, n_atoms), F32),
            pltpu.SMEM(block_counts.shape, jnp.int32),
            pltpu.SMEM((NNB, NB), jnp.int32),
            pltpu.VMEM(integer_wave_vectors.shape, jnp.int32),
            pltpu.VMEM((16, 16), BF16),
            dma((7,)),
            pltpu.VMEM((NB + 4, 25, 16, BS), BF16),
            pltpu.VMEM((16, n_atoms), BF16),
            pltpu.VMEM((NB, 48, BS), BF16),
            pltpu.VMEM((4, 48, BS), BF16),
            pltpu.VMEM((NB + 4, 48, BS), BF16),
            pltpu.VMEM((NB, 32, BS), BF16),
            pltpu.VMEM((NB, NNB, BS, BS), BF16),
            pltpu.VMEM((NB, 1, BS), F32),
            pltpu.VMEM((NI, NB, 16, BS), BF16),
            pltpu.VMEM((NI, 16, 16), BF16),
            pltpu.VMEM((NG, 8, 128), F32),
            pltpu.VMEM((NG, 8, 128), F32),
            pltpu.VMEM((NR, 8, 128), F32),
            dma((NB,)),
            dma,
            pltpu.SemaphoreType.REGULAR((3,)),
            dma((4,)),
            dma((4,)),
            dma((2, NX - 1)),
            dma((2, NX - 1)),
            dma((2, NX)),
            dma((2, NX)),
            dma((NI - 1,)),
            dma((NI - 1,)),
            dma((NG - 1,)),
            dma((NG - 1,)),
            dma((NR - 1,)),
            dma((NR - 1,)),
            dma((NG - 1,)),
            dma((NG - 1,)),
            dma((NX - 1,)),
            dma((NX - 1,)),
            dma((NX,)),
            dma((NX,)),
        ],
        compiler_params=pltpu.CompilerParams(
            collective_id=0, has_side_effects=True, vmem_limit_bytes=56 << 20
        ),
    )(
        queries,
        key_states,
        fractional,
        block_counts,
        neighbors.T,
        integer_wave_vectors,
        charge_weight,
        value_states.transpose(1, 0, 2),
    )
    attention, potential, forces = pl.pallas_call(
        field,
        out_shape=(
            att_shape,
            jax.ShapeDtypeStruct((16, n_atoms), F32),
            jax.ShapeDtypeStruct((3, n_atoms), F32),
        ),
        in_specs=[hbm] * 6,
        out_specs=(hbm, vmem, vmem),
        scratch_shapes=[pltpu.VMEM(att_shape.shape, BF16)]
        + slots
        + [pltpu.VMEM((NI, 96, 256), BF16), dma((7,))],
        compiler_params=pltpu.CompilerParams(vmem_limit_bytes=56 << 20),
    )(*made)
    return attention.transpose(1, 0, 2), potential, forces


def solution(mesh):
    torus = Mesh(mesh.devices.reshape(NY, NZ, NX, NC), ("y", "z", "x", "c"))
    return jax.shard_map(
        local,
        mesh=torus,
        in_specs=(
            P(INNER, None, SEQ),
            P(INNER, None, SEQ),
            P(INNER, None, SEQ),
            P(None, SEQ),
            P(),
            P(SEQ, None),
            P(),
            P(INNER, None),
        ),
        out_specs=(P(INNER, None, SEQ), P(None, SEQ), P(None, SEQ)),
        check_vma=False,
    )
```

```python
import jax
import jax.numpy as jnp
from jax import lax
from jax.experimental import pallas as pl
from jax.experimental.pallas import tpu as pltpu
from jax.sharding import Mesh
from jax.sharding import PartitionSpec as P

BS = 256
NNB = 3
NY, NZ, NX, NC = 4, 32, 4, 2
SEQ = ("y", "z")
INNER = ("x", "c")
NI = NX * NC
NSEQ = NY * NZ
GZ = 2
NG = NY * GZ
NR = NZ // GZ
NB = 8
F32, BF16 = jnp.float32, jnp.bfloat16
MESH = pl.DeviceIdType.MESH
DEAD = -1e30

ewald_scale = 40.0
ewald_damp = 0.02

COS = (1.0, -19.739208221435547, 64.93939208984375, -85.45665740966797, 60.242130279541016, -26.4046688079834, 7.800131320953369, -1.4531123638153076)
SIN = (6.2831854820251465, -41.34170150756836, 81.6052474975586, -76.70575714111328, 42.057369232177734, -15.084554672241211, 3.7759575843811035, -0.6150599718093872)


def poly(coeffs, u):
    y = jnp.full_like(u, coeffs[-1])
    for k in coeffs[-2::-1]:
        y = y * u + k
    return y


def cos_sin_turns(t):
    r = t - jnp.floor(t + 0.5)
    u = r * r
    return poly(COS, u), poly(SIN, u) * r


def nt(a, b):
    return lax.dot_general(a, b, (((1,), (1,)), ((), ())), preferred_element_type=F32)


def tn(a, b):
    return lax.dot_general(a, b, (((0,), (0,)), ((), ())), preferred_element_type=F32)


def nn(a, b):
    return jnp.dot(a, b, preferred_element_type=F32)


def listed_at(nbr, g, j, low, high):
    return jnp.clip(nbr[j, g] - low, 0, high)


def kernel(
    q_hbm, k_hbm, frac_hbm, counts_hbm, nbr_hbm, iwv_hbm, cw_hbm, v_hbm,
    att_hbm, gt_hbm, wt_hbm, xt_hbm, bt_hbm, chg_hbm,
    ob, gt, wt, xt, bt, chg, sem_o,
    q, k, frac, counts, nbr, iwv, cw, sem_i, v2, v0, ks, kin, kb, qs, ps, rden, a0, cwa, gs, rs, os_,
    sem_v, sem_v0, known, halo_s, halo_r, a_s, a_r, af_s, af_r, c_s, c_r, r_s, r_r, f_s, f_r, t_s, t_r, g_s, g_r, gf_s, gf_r,
):
    y, z, x, c = (lax.axis_index(a) for a in ("y", "z", "x", "c"))
    inner = x * NC + c
    seq = y * NZ + z
    gid = y * GZ + lax.rem(z, GZ)
    rid = z // GZ
    first = seq * NB

    def at_seq(s):
        return {"y": s // NZ, "z": lax.rem(s, NZ)}

    right = at_seq(lax.rem(seq + 1, NSEQ))
    left = at_seq(lax.rem(seq + NSEQ - 1, NSEQ))
    other = {"c": 1 - c}

    def inner_peer(o):
        p = lax.rem(inner + o, NI)
        return {"x": p // NC, "c": lax.rem(p, NC)}

    def x_peer(o):
        return {"x": lax.rem(x + o, NX)}

    def x_from(o):
        return lax.rem(x + NX - o, NX) * NC + c

    def group_peer(o):
        p = lax.rem(gid + o, NG)
        return p, {"y": p // GZ, "z": rid * GZ + lax.rem(p, GZ)}

    def ring_peer(o):
        p = lax.rem(rid + o, NR)
        return {"z": p * GZ + lax.rem(z, GZ)}

    pairs = ((k_hbm, k), (counts_hbm, counts), (q_hbm, q), (cw_hbm, cw), (nbr_hbm, nbr), (frac_hbm, frac), (iwv_hbm, iwv))
    takes = [pltpu.make_async_copy(a, b, sem_i.at[i]) for i, (a, b) in enumerate(pairs)]
    load_v0 = pltpu.make_async_copy(v_hbm.at[0], v0, sem_v0)
    for cp in takes[:2] + [load_v0] + takes[2:]:
        cp.start()

    barrier = pltpu.get_barrier_semaphore()
    near = [left, right, ring_peer(1), ring_peer(NR - 1)]
    near += [inner_peer(o) for o in range(1, NI)]
    near += [group_peer(o)[1] for o in range(1, NG)]
    for p in near:
        pl.semaphore_signal(barrier, inc=1, device_id=p, device_id_type=MESH)

    def tell(r):
        for o in (1 << r, NR - (1 << r)):
            pl.semaphore_signal(known.at[r], inc=1, device_id=ring_peer(o), device_id_type=MESH)

    def hear(r):
        pl.semaphore_wait(known.at[r], 2)

    loads = []
    for b in (0, 1, 6, 7, 2, 3, 4, 5):
        cp = pltpu.make_async_copy(v_hbm.at[:, :, pl.ds(b * BS, BS)], v2.at[b + 2], sem_v.at[b])
        cp.start()
        loads.append(cp)

    for cp in takes[:5]:
        cp.wait()

    row16 = lax.broadcasted_iota(jnp.int32, (16, BS), 0)
    lane16 = lax.broadcasted_iota(jnp.int32, (16, BS), 1)
    for b in range(NB):
        cols = pl.ds(b * BS, BS)
        live = lane16 < counts[first + b]
        bias = jnp.where((row16 == 0) & jnp.logical_not(live), DEAD, 0.0)
        ks[b, 0:16, :] = k[0, :, cols]
        ks[b, 16:32, :] = bias.astype(BF16)
        qs[b, 0:16, :] = (q[0, :, cols].astype(F32) * 0.25).astype(BF16)
        qs[b, 16:32, :] = jnp.where(row16 == 0, 1.0, 0.0).astype(BF16)
    cwa[inner] = cw[...]
    load_v0.wait()
    for b in range(NB):
        ks[b, 32:48, :] = v0[:, b * BS : (b + 1) * BS]

    def send(src, dst, ssem, rsem, dev):
        cp = pltpu.make_async_remote_copy(
            src_ref=src, dst_ref=dst, send_sem=ssem, recv_sem=rsem, device_id=dev, device_id_type=MESH
        )
        cp.start()
        return cp

    pl.semaphore_wait(barrier, len(near))
    kh = [
        send(ks.at[pl.ds(6, 2)], kin.at[pl.ds(0, 2)], halo_s.at[0], halo_r.at[0], right),
        send(ks.at[pl.ds(0, 2)], kin.at[pl.ds(2, 2)], halo_s.at[1], halo_r.at[1], left),
    ]
    tell(0)
    cws = [
        send(cwa.at[inner], cwa.at[inner], c_s.at[o - 1], c_r.at[o - 1], inner_peer(o))
        for o in range(1, NI)
    ]
    for cp in loads[:4]:
        cp.wait()
    vh = [
        send(v2.at[pl.ds(8, 2)], v2.at[pl.ds(0, 2)], halo_s.at[2], halo_r.at[2], right),
        send(v2.at[pl.ds(2, 2)], v2.at[pl.ds(10, 2)], halo_s.at[3], halo_r.at[3], left),
    ]

    def attend(src, low, high, at):
        g = lax.rem(at + 2, NB)
        listed = [listed_at(nbr, g, j, low, high) for j in range(NNB)]
        qa = qs[g]
        s = [tn(src[i, 0:32, :], qa) for i in listed]
        m = s[0].max(axis=0, keepdims=True)
        for t in s[1:]:
            m = jnp.maximum(m, t.max(axis=0, keepdims=True))
        den = jnp.zeros((1, BS), F32)
        acc = jnp.zeros((16, BS), F32)
        for j, i in enumerate(listed):
            w = jnp.exp(s[j] - m)
            den += w.sum(axis=0, keepdims=True)
            wb = w.astype(BF16)
            ps[g, j] = wb
            acc += nn(src[i, 32:48, :], wb)
        live_q = lax.broadcasted_iota(jnp.int32, (1, BS), 1) < counts[first + g]
        rd = jnp.where(live_q, 1.0 / den, 0.0)
        rden[g] = rd
        a0[inner, at] = (acc * rd).astype(BF16)

    def spread(half):
        mine = a0.at[inner, pl.ds(4 * half, 4)]
        out = [send(mine, mine, a_s.at[half, o - 1], a_r.at[half, o - 1], x_peer(o)) for o in range(1, NX)]
        return out, [send(mine, mine, af_s.at[half, 0], af_r.at[half, 0], other)]

    def pass_on(half, out, on):
        for o in range(1, NX):
            out[o - 1].wait_recv()
            got = a0.at[x_from(o), pl.ds(4 * half, 4)]
            on.append(send(got, got, af_s.at[half, o], af_r.at[half, o], other))

    @pl.loop(0, 4)
    def _(at):
        attend(ks, first, NB - 1, at)

    out0, on0 = spread(0)
    for cp in kh:
        cp.wait_recv()
    hear(0)
    tell(1)
    kb[0:2] = kin[0:2]
    kb[2:10] = ks[...]
    kb[10:12] = kin[2:4]

    @pl.loop(4, 8)
    def _(at):
        attend(kb, first - 2, NB + 3, at)

    out1, on1 = spread(1)
    pass_on(0, out0, on0)
    hear(1)
    tell(2)

    for cp in takes[5:]:
        cp.wait()

    n_atoms = NB * BS
    iota8 = lax.broadcasted_iota(jnp.int32, (8, n_atoms), 0).astype(F32)
    xc, xs = cos_sin_turns(frac[0:1, :] * iota8)
    xt[0] = xc
    xt[1] = xs
    u_tab = cos_sin_turns(frac[1:2, :] * iota8)
    v_tab = cos_sin_turns(frac[2:3, :] * iota8)
    for u in range(2):
        for v in range(2):
            for n in range(0, 8, 2):
                lo = u_tab[u][n : n + 1, :] * v_tab[v]
                hi = u_tab[u][n + 1 : n + 2, :] * v_tab[v]
                at = u * 128 + v * 64 + n * 8
                bt[at : at + 16, :] = jnp.concatenate([lo, hi], axis=0).astype(BF16)

    stored = []

    def store(i, src, dst):
        cp = pltpu.make_async_copy(src, dst, sem_o.at[i])
        cp.start()
        stored.append(cp)

    store(0, bt, bt_hbm)
    store(1, xt, xt_hbm)

    def charge(at):
        g = (at + 2) % NB
        r = tn(cwa[...].reshape(NI * 16, 16), a0[:, at].reshape(NI * 16, BS))
        chg[:, g * BS : (g + 1) * BS] = r

    def structure(low, high):
        cols = slice(low * BS, high * BS)
        charges = chg[:, cols]
        own_c = xt[0, pl.ds(inner, 1), cols]
        own_s = xt[1, pl.ds(inner, 1), cols]
        amp = jnp.concatenate([charges * own_c, charges * own_s], axis=0) * (1.0 / 512.0)
        amp_h = amp.astype(BF16)
        amp_l = (amp - amp_h.astype(F32)).astype(BF16)
        both = nt(jnp.concatenate([amp_h, amp_l], axis=0), bt[:, cols])
        return both[0:32] + both[32:64]

    for cp in cws + on0:
        cp.wait_recv()
    for at in range(4):
        charge(at)
    part = structure(2, 6)
    pass_on(1, out1, on1)
    for cp in on1:
        cp.wait_recv()
    for at in range(4, 8):
        charge(at)
    part += structure(0, 2) + structure(6, 8)
    store(2, chg, chg_hbm)
    for p in range(8):
        gs[p] = part[(p // 2) * 8 : (p // 2) * 8 + 8, (p % 2) * 128 : (p % 2) * 128 + 128]

    rsend = []
    for o in range(1, NG):
        p, dev = group_peer(o)
        rsend.append(send(gs.at[p], rs.at[gid], r_s.at[o - 1], r_r.at[o - 1], dev))
    rs[gid] = gs[gid]
    hear(2)
    for cp in rsend:
        cp.wait_recv()
    os_[rid] = jnp.sum(rs[...], axis=0)
    fsend = [
        send(os_.at[rid], os_.at[rid], f_s.at[o - 1], f_r.at[o - 1], ring_peer(o))
        for o in sorted(range(1, NR), key=lambda o: abs(o - NR // 2))
    ]

    n0, n1, n2 = iwv[0:1, :], iwv[1:2, :], iwv[2:3, :]
    n_waves = iwv.shape[1]
    flip = n0 < 0
    n1 = jnp.where(flip, -n1, n1)
    n2 = jnp.where(flip, -n2, n2)
    s1 = jnp.where(n1 < 0, -1.0, 1.0)
    s2 = jnp.where(n2 < 0, -1.0, 1.0)
    place = jnp.abs(n1) * 8 + jnp.abs(n2)
    rows128 = lax.broadcasted_iota(jnp.int32, (128, n_waves), 0)
    hot = jnp.where((rows128 & 63) == place, 1.0, 0.0).astype(BF16)
    mine = lax.broadcasted_iota(jnp.int32, (8, n_waves), 0) == jnp.abs(n0)
    coeffs = [jnp.ones_like(s1), s1, s2, s1 * s2]
    listed = jnp.concatenate([jnp.where(mine, cf, 0.0) for cf in coeffs], axis=0).astype(BF16)
    cnt = nt(listed, hot)
    d_row = lax.broadcasted_iota(jnp.int32, (8, 128), 0)
    l_row = lax.broadcasted_iota(jnp.int32, (8, 128), 1)
    b_row = (l_row & 63) >> 3
    g_row = l_row & 7
    norm2 = jnp.maximum(d_row * d_row + b_row * b_row + g_row * g_row, 1).astype(F32)
    kw = ewald_scale * jnp.exp(-ewald_damp * norm2) / norm2
    for t in range(4):
        wt[t] = cnt[t * 8 : (t + 1) * 8] * kw
    store(3, wt, wt_hbm)

    for cp in loads[4:]:
        cp.wait()
    for cp in vh:
        cp.wait_recv()

    @pl.loop(0, NB)
    def _(g):
        acc = jnp.zeros((400, BS), F32)
        for j in range(NNB):
            i = listed_at(nbr, g, j, first - 2, NB + 3)
            acc += nn(v2[i].reshape(400, BS), ps[g, j])
        ob[:, :, pl.ds(pl.multiple_of(g * BS, BS), BS)] = (acc * rden[g]).astype(BF16).reshape(25, 16, BS)

    store(4, ob, att_hbm)

    for cp in fsend:
        cp.wait_recv()
    gt[inner, gid] = jnp.sum(os_[...], axis=0)
    tsend = [
        send(gt.at[inner, gid], gt.at[inner, gid], t_s.at[o - 1], t_r.at[o - 1], group_peer(o)[1])
        for o in range(1, NG)
    ]
    for cp in tsend:
        cp.wait_recv()
    gsend = [send(gt.at[inner], gt.at[inner], g_s.at[o - 1], g_r.at[o - 1], x_peer(o)) for o in range(1, NX)]
    gon = [send(gt.at[inner], gt.at[inner], gf_s.at[0], gf_r.at[0], other)]
    for o in range(1, NX):
        gsend[o - 1].wait_recv()
        got = gt.at[x_from(o)]
        gon.append(send(got, got, gf_s.at[o], gf_r.at[o], other))
    for cp in gon:
        cp.wait_recv()
    store(5, gt, gt_hbm)
    for cp in kh + cws + vh + out0 + on0 + out1 + on1 + rsend + fsend + tsend + gsend + gon:
        cp.wait_send()
    for cp in stored:
        cp.wait()


def field(
    att_hbm, gt_hbm, wt_hbm, xt_hbm, bt_hbm, chg_hbm, o_att, o_pot, o_for, att, gt, wt, xt, bt, chg, hs, sem
):
    pairs = ((gt_hbm, gt), (wt_hbm, wt), (bt_hbm, bt), (xt_hbm, xt), (chg_hbm, chg), (att_hbm, att))
    takes = [pltpu.make_async_copy(a, b, sem.at[i]) for i, (a, b) in enumerate(pairs)]
    for cp in takes:
        cp.start()
    for cp in takes[:2]:
        cp.wait()

    lane = lax.broadcasted_iota(jnp.int32, (1, 128), 1)
    sgn = jnp.where(lane < 64, -1.0, 1.0)
    w_n1 = ((lane & 63) >> 3).astype(F32)
    w_n2 = (lane & 7).astype(F32)

    def swap(a):
        return pltpu.roll(a, 64, 1)

    for d in range(NI):
        w0, w1, w2, w12 = (wt[t, d : d + 1, :] for t in range(4))
        g4 = {
            (p, u): jnp.concatenate([gt[d, 4 * p + u], gt[d, 4 * p + 2 + u]], axis=0)
            for p in range(2)
            for u in range(2)
        }
        h = {}
        for p in range(2):
            for u in range(2):
                su = sgn if u == 0 else -sgn
                sp = sgn if p == 0 else -sgn
                pu = -1.0 if p == u else 1.0
                h[p, u] = (
                    w0 * g4[p, u]
                    + (su * w12) * swap(g4[p, 1 - u])
                    + (pu * w1) * g4[1 - p, 1 - u]
                    + (sp * w2) * swap(g4[1 - p, u])
                )
        for p in range(2):
            r = p * 16
            hs[d, r : r + 16, 0:128] = h[p, 0].astype(BF16)
            hs[d, r : r + 16, 128:256] = h[p, 1].astype(BF16)
            hs[d, 32 + r : 48 + r, 0:128] = (-w_n1 * h[p, 1]).astype(BF16)
            hs[d, 32 + r : 48 + r, 128:256] = (w_n1 * h[p, 0]).astype(BF16)
            for u in range(2):
                hs[d, 64 + r : 80 + r, u * 128 : u * 128 + 128] = (
                    (w_n2 * sgn) * swap(h[p, u])
                ).astype(BF16)

    for cp in takes[2:5]:
        cp.wait()

    def part(t):
        cols = pl.ds(pl.multiple_of(t * BS, BS), BS)
        basis = bt[:, cols]
        pot = jnp.zeros((16, BS), F32)
        fx = jnp.zeros((16, BS), F32)
        fy = jnp.zeros((16, BS), F32)
        fz = jnp.zeros((16, BS), F32)
        every = nn(hs[...].reshape(NI * 96, 256), basis)
        for d in range(NI):
            r = every[d * 96 : (d + 1) * 96]
            xc = xt[0, d : d + 1, cols]
            xs = xt[1, d : d + 1, cols]
            pot += xc * r[0:16] + xs * r[16:32]
            if d:
                fx += (d * xs) * r[0:16] - (d * xc) * r[16:32]
            fy += xc * r[32:48] + xs * r[48:64]
            fz += xc * r[64:80] + xs * r[80:96]
        o_pot[:, cols] = pot
        ch = chg[:, cols]
        for i, f in enumerate((fx, fy, fz)):
            o_for[i : i + 1, cols] = jnp.sum(ch * f, axis=0, keepdims=True)

    pl.loop(0, NB // 2)(part)
    takes[5].wait()
    give = pltpu.make_async_copy(att, o_att, sem.at[6])
    give.start()
    pl.loop(NB // 2, NB)(part)
    give.wait()


def local(queries, key_states, value_states, fractional, block_counts, neighbors, integer_wave_vectors, charge_weight):
    n_atoms = queries.shape[2]
    vmem = pl.BlockSpec(memory_space=pltpu.VMEM)
    hbm = pl.BlockSpec(memory_space=pltpu.HBM)
    dma = pltpu.SemaphoreType.DMA
    att_shape = jax.ShapeDtypeStruct((25, 16, n_atoms), BF16)
    passed = (
        jax.ShapeDtypeStruct((NI, NG, 8, 128), F32),
        jax.ShapeDtypeStruct((4, 8, 128), F32),
        jax.ShapeDtypeStruct((2, 8, n_atoms), F32),
        jax.ShapeDtypeStruct((256, n_atoms), BF16),
        jax.ShapeDtypeStruct((16, n_atoms), F32),
    )
    slots = [pltpu.VMEM(t.shape, t.dtype) for t in passed]
    made = pl.pallas_call(
        kernel,
        out_shape=(att_shape,) + passed,
        in_specs=[hbm] * 8,
        out_specs=(hbm,) * 6,
        scratch_shapes=[pltpu.VMEM(att_shape.shape, BF16)]
        + slots
        + [
            dma((6,)),
            pltpu.VMEM((1, 16, n_atoms), BF16),
            pltpu.VMEM((1, 16, n_atoms), BF16),
            pltpu.VMEM((3, n_atoms), F32),
            pltpu.SMEM(block_counts.shape, jnp.int32),
            pltpu.SMEM((NNB, NB), jnp.int32),
            pltpu.VMEM(integer_wave_vectors.shape, jnp.int32),
            pltpu.VMEM((16, 16), BF16),
            dma((7,)),
            pltpu.VMEM((NB + 4, 25, 16, BS), BF16),
            pltpu.VMEM((16, n_atoms), BF16),
            pltpu.VMEM((NB, 48, BS), BF16),
            pltpu.VMEM((4, 48, BS), BF16),
            pltpu.VMEM((NB + 4, 48, BS), BF16),
            pltpu.VMEM((NB, 32, BS), BF16),
            pltpu.VMEM((NB, NNB, BS, BS), BF16),
            pltpu.VMEM((NB, 1, BS), F32),
            pltpu.VMEM((NI, NB, 16, BS), BF16),
            pltpu.VMEM((NI, 16, 16), BF16),
            pltpu.VMEM((NG, 8, 128), F32),
            pltpu.VMEM((NG, 8, 128), F32),
            pltpu.VMEM((NR, 8, 128), F32),
            dma((NB,)),
            dma,
            pltpu.SemaphoreType.REGULAR((3,)),
            dma((4,)),
            dma((4,)),
            dma((2, NX - 1)),
            dma((2, NX - 1)),
            dma((2, NX)),
            dma((2, NX)),
            dma((NI - 1,)),
            dma((NI - 1,)),
            dma((NG - 1,)),
            dma((NG - 1,)),
            dma((NR - 1,)),
            dma((NR - 1,)),
            dma((NG - 1,)),
            dma((NG - 1,)),
            dma((NX - 1,)),
            dma((NX - 1,)),
            dma((NX,)),
            dma((NX,)),
        ],
        compiler_params=pltpu.CompilerParams(
            collective_id=0, has_side_effects=True, vmem_limit_bytes=56 << 20
        ),
    )(
        queries,
        key_states,
        fractional,
        block_counts,
        neighbors.T,
        integer_wave_vectors,
        charge_weight,
        value_states.transpose(1, 0, 2),
    )
    attention, potential, forces = pl.pallas_call(
        field,
        out_shape=(
            att_shape,
            jax.ShapeDtypeStruct((16, n_atoms), F32),
            jax.ShapeDtypeStruct((3, n_atoms), F32),
        ),
        in_specs=[hbm] * 6,
        out_specs=(hbm, vmem, vmem),
        scratch_shapes=[pltpu.VMEM(att_shape.shape, BF16)]
        + slots
        + [pltpu.VMEM((NI, 96, 256), BF16), dma((7,))],
        compiler_params=pltpu.CompilerParams(vmem_limit_bytes=56 << 20),
    )(*made)
    return attention.transpose(1, 0, 2), potential, forces


def solution(mesh):
    torus = Mesh(mesh.devices.reshape(NY, NZ, NX, NC), ("y", "z", "x", "c"))
    return jax.shard_map(
        local,
        mesh=torus,
        in_specs=(
            P(INNER, None, SEQ),
            P(INNER, None, SEQ),
            P(INNER, None, SEQ),
            P(None, SEQ),
            P(),
            P(SEQ, None),
            P(),
            P(INNER, None),
        ),
        out_specs=(P(INNER, None, SEQ), P(None, SEQ), P(None, SEQ)),
        check_vma=False,
    )
```

```python
import jax
import jax.numpy as jnp
from jax import lax
from jax.experimental import pallas as pl
from jax.experimental.pallas import tpu as pltpu
from jax.sharding import Mesh
from jax.sharding import PartitionSpec as P

BS = 256
NNB = 3
NY, NZ, NX, NC = 4, 32, 4, 2
SEQ = ("y", "z")
INNER = ("x", "c")
NI = NX * NC
NSEQ = NY * NZ
GZ = 2
NG = NY * GZ
NR = NZ // GZ
NB = 8
F32, BF16 = jnp.float32, jnp.bfloat16
MESH = pl.DeviceIdType.MESH
DEAD = -1e30

ewald_scale = 40.0
ewald_damp = 0.02

COS = (1.0, -19.739208221435547, 64.93939208984375, -85.45665740966797, 60.242130279541016, -26.4046688079834, 7.800131320953369, -1.4531123638153076)
SIN = (6.2831854820251465, -41.34170150756836, 81.6052474975586, -76.70575714111328, 42.057369232177734, -15.084554672241211, 3.7759575843811035, -0.6150599718093872)


def poly(coeffs, u):
    y = jnp.full_like(u, coeffs[-1])
    for k in coeffs[-2::-1]:
        y = y * u + k
    return y


def cos_sin_turns(t):
    r = t - jnp.floor(t + 0.5)
    u = r * r
    return poly(COS, u), poly(SIN, u) * r


def nt(a, b):
    return lax.dot_general(a, b, (((1,), (1,)), ((), ())), preferred_element_type=F32)


def tn(a, b):
    return lax.dot_general(a, b, (((0,), (0,)), ((), ())), preferred_element_type=F32)


def nn(a, b):
    return jnp.dot(a, b, preferred_element_type=F32)


def listed_at(nbr, g, j, low, high):
    return jnp.clip(nbr[j, g] - low, 0, high)


def kernel(
    q_hbm, k_hbm, frac_hbm, counts_hbm, nbr_hbm, iwv_hbm, cw_hbm, v_hbm,
    att_hbm, gt_hbm, wt_hbm, xt_hbm, bt_hbm, chg_hbm,
    ob, gt, wt, xt, bt, chg, sem_o,
    q, k, frac, counts, nbr, iwv, cw, sem_i, v2, v0, ks, kin, kb, qs, ps, rden, a0, cwa, gs, rs, os_,
    sem_v, sem_v0, known, halo_s, halo_r, a_s, a_r, af_s, af_r, c_s, c_r, r_s, r_r, f_s, f_r, t_s, t_r, g_s, g_r, gf_s, gf_r,
):
    y, z, x, c = (lax.axis_index(a) for a in ("y", "z", "x", "c"))
    inner = x * NC + c
    seq = y * NZ + z
    gid = y * GZ + lax.rem(z, GZ)
    rid = z // GZ
    first = seq * NB

    def at_seq(s):
        return {"y": s // NZ, "z": lax.rem(s, NZ)}

    right = at_seq(lax.rem(seq + 1, NSEQ))
    left = at_seq(lax.rem(seq + NSEQ - 1, NSEQ))
    other = {"c": 1 - c}

    def inner_peer(o):
        p = lax.rem(inner + o, NI)
        return {"x": p // NC, "c": lax.rem(p, NC)}

    def x_peer(o):
        return {"x": lax.rem(x + o, NX)}

    def x_from(o):
        return lax.rem(x + NX - o, NX) * NC + c

    def group_peer(o):
        p = lax.rem(gid + o, NG)
        return p, {"y": p // GZ, "z": rid * GZ + lax.rem(p, GZ)}

    def ring_peer(o):
        p = lax.rem(rid + o, NR)
        return {"z": p * GZ + lax.rem(z, GZ)}

    pairs = ((k_hbm, k), (counts_hbm, counts), (q_hbm, q), (cw_hbm, cw), (nbr_hbm, nbr), (frac_hbm, frac), (iwv_hbm, iwv))
    takes = [pltpu.make_async_copy(a, b, sem_i.at[i]) for i, (a, b) in enumerate(pairs)]
    load_v0 = pltpu.make_async_copy(v_hbm.at[0], v0, sem_v0)
    for cp in takes[:2] + [load_v0] + takes[2:]:
        cp.start()

    barrier = pltpu.get_barrier_semaphore()
    near = [left, right, ring_peer(1), ring_peer(NR - 1)]
    near += [inner_peer(o) for o in range(1, NI)]
    near += [group_peer(o)[1] for o in range(1, NG)]
    for p in near:
        pl.semaphore_signal(barrier, inc=1, device_id=p, device_id_type=MESH)

    def tell(r):
        for o in (1 << r, NR - (1 << r)):
            pl.semaphore_signal(known.at[r], inc=1, device_id=ring_peer(o), device_id_type=MESH)

    def hear(r):
        pl.semaphore_wait(known.at[r], 2)

    loads = []
    for b in (0, 1, 6, 7, 2, 3, 4, 5):
        cp = pltpu.make_async_copy(v_hbm.at[:, :, pl.ds(b * BS, BS)], v2.at[b + 2], sem_v.at[b])
        cp.start()
        loads.append(cp)

    for cp in takes[:2]:
        cp.wait()

    row16 = lax.broadcasted_iota(jnp.int32, (16, BS), 0)
    lane16 = lax.broadcasted_iota(jnp.int32, (16, BS), 1)
    def build(b):
        cols = pl.ds(b * BS, BS)
        live = lane16 < counts[first + b]
        bias = jnp.where((row16 == 0) & jnp.logical_not(live), DEAD, 0.0)
        ks[b, 0:16, :] = k[0, :, cols]
        ks[b, 16:32, :] = bias.astype(BF16)
        ks[b, 32:48, :] = v0[:, b * BS : (b + 1) * BS]

    load_v0.wait()
    for b in (0, 1, 6, 7):
        build(b)

    def send(src, dst, ssem, rsem, dev):
        cp = pltpu.make_async_remote_copy(
            src_ref=src, dst_ref=dst, send_sem=ssem, recv_sem=rsem, device_id=dev, device_id_type=MESH
        )
        cp.start()
        return cp

    pl.semaphore_wait(barrier, len(near))
    kh = [
        send(ks.at[pl.ds(6, 2)], kin.at[pl.ds(0, 2)], halo_s.at[0], halo_r.at[0], right),
        send(ks.at[pl.ds(0, 2)], kin.at[pl.ds(2, 2)], halo_s.at[1], halo_r.at[1], left),
    ]
    tell(0)
    for cp in takes[2:5]:
        cp.wait()
    cwa[inner] = cw[...]
    cws = [
        send(cwa.at[inner], cwa.at[inner], c_s.at[o - 1], c_r.at[o - 1], inner_peer(o))
        for o in range(1, NI)
    ]
    for b in (2, 3, 4, 5):
        build(b)
    for b in range(NB):
        qs[b, 0:16, :] = (q[0, :, b * BS : (b + 1) * BS].astype(F32) * 0.25).astype(BF16)
        qs[b, 16:32, :] = jnp.where(row16 == 0, 1.0, 0.0).astype(BF16)
    for cp in loads[:4]:
        cp.wait()
    vh = [
        send(v2.at[pl.ds(8, 2)], v2.at[pl.ds(0, 2)], halo_s.at[2], halo_r.at[2], right),
        send(v2.at[pl.ds(2, 2)], v2.at[pl.ds(10, 2)], halo_s.at[3], halo_r.at[3], left),
    ]

    def attend(src, low, high, at):
        g = lax.rem(at + 2, NB)
        listed = [listed_at(nbr, g, j, low, high) for j in range(NNB)]
        qa = qs[g]
        s = [tn(src[i, 0:32, :], qa) for i in listed]
        m = s[0].max(axis=0, keepdims=True)
        for t in s[1:]:
            m = jnp.maximum(m, t.max(axis=0, keepdims=True))
        den = jnp.zeros((1, BS), F32)
        acc = jnp.zeros((16, BS), F32)
        for j, i in enumerate(listed):
            w = jnp.exp(s[j] - m)
            den += w.sum(axis=0, keepdims=True)
            wb = w.astype(BF16)
            ps[g, j] = wb
            acc += nn(src[i, 32:48, :], wb)
        live_q = lax.broadcasted_iota(jnp.int32, (1, BS), 1) < counts[first + g]
        rd = jnp.where(live_q, 1.0 / den, 0.0)
        rden[g] = rd
        a0[inner, at] = (acc * rd).astype(BF16)

    pieces = (pl.ds(0, 4), pl.ds(4, 2), pl.ds(6, 2))

    def spread(i):
        mine = a0.at[inner, pieces[i]]
        out = [send(mine, mine, a_s.at[i, o - 1], a_r.at[i, o - 1], x_peer(o)) for o in range(1, NX)]
        return out, [send(mine, mine, af_s.at[i, 0], af_r.at[i, 0], other)]

    def pass_on(i, out, on):
        for o in range(1, NX):
            out[o - 1].wait_recv()
            got = a0.at[x_from(o), pieces[i]]
            on.append(send(got, got, af_s.at[i, o], af_r.at[i, o], other))

    @pl.loop(0, 4, unroll=2)
    def _(at):
        attend(ks, first, NB - 1, at)

    out0, on0 = spread(0)
    for cp in kh:
        cp.wait_recv()
    hear(0)
    tell(1)
    kb[0:2] = kin[0:2]
    kb[2:10] = ks[...]
    kb[10:12] = kin[2:4]

    @pl.loop(4, 6, unroll=2)
    def _(at):
        attend(kb, first - 2, NB + 3, at)

    out1, on1 = spread(1)

    @pl.loop(6, 8, unroll=2)
    def _(at):
        attend(kb, first - 2, NB + 3, at)

    out2, on2 = spread(2)
    pass_on(0, out0, on0)
    hear(1)
    tell(2)

    for cp in takes[5:]:
        cp.wait()

    n_atoms = NB * BS
    iota8 = lax.broadcasted_iota(jnp.int32, (8, n_atoms), 0).astype(F32)
    xc, xs = cos_sin_turns(frac[0:1, :] * iota8)
    xt[0] = xc
    xt[1] = xs
    u_tab = cos_sin_turns(frac[1:2, :] * iota8)
    v_tab = cos_sin_turns(frac[2:3, :] * iota8)
    for u in range(2):
        for v in range(2):
            for n in range(0, 8, 2):
                lo = u_tab[u][n : n + 1, :] * v_tab[v]
                hi = u_tab[u][n + 1 : n + 2, :] * v_tab[v]
                at = u * 128 + v * 64 + n * 8
                bt[at : at + 16, :] = jnp.concatenate([lo, hi], axis=0).astype(BF16)

    stored = []

    def store(i, src, dst):
        cp = pltpu.make_async_copy(src, dst, sem_o.at[i])
        cp.start()
        stored.append(cp)

    store(0, bt, bt_hbm)
    store(1, xt, xt_hbm)

    def charge(at):
        g = (at + 2) % NB
        r = tn(cwa[...].reshape(NI * 16, 16), a0[:, at].reshape(NI * 16, BS))
        chg[:, g * BS : (g + 1) * BS] = r

    def structure(low, high):
        cols = slice(low * BS, high * BS)
        charges = chg[:, cols]
        own_c = xt[0, pl.ds(inner, 1), cols]
        own_s = xt[1, pl.ds(inner, 1), cols]
        amp = jnp.concatenate([charges * own_c, charges * own_s], axis=0) * (1.0 / 512.0)
        amp_h = amp.astype(BF16)
        amp_l = (amp - amp_h.astype(F32)).astype(BF16)
        both = nt(jnp.concatenate([amp_h, amp_l], axis=0), bt[:, cols])
        return both[0:32] + both[32:64]

    for cp in cws + on0:
        cp.wait_recv()
    for at in range(4):
        charge(at)
    part = structure(2, 6)
    pass_on(1, out1, on1)
    pass_on(2, out2, on2)
    for cp in on1 + on2:
        cp.wait_recv()
    for at in range(4, 8):
        charge(at)
    part += structure(0, 2) + structure(6, 8)
    store(2, chg, chg_hbm)
    for p in range(8):
        gs[p] = part[(p // 2) * 8 : (p // 2) * 8 + 8, (p % 2) * 128 : (p % 2) * 128 + 128]

    rsend = []
    for o in range(1, NG):
        p, dev = group_peer(o)
        rsend.append(send(gs.at[p], rs.at[gid], r_s.at[o - 1], r_r.at[o - 1], dev))
    rs[gid] = gs[gid]
    hear(2)
    for cp in rsend:
        cp.wait_recv()
    os_[rid] = jnp.sum(rs[...], axis=0)
    fsend = [
        send(os_.at[rid], os_.at[rid], f_s.at[o - 1], f_r.at[o - 1], ring_peer(o))
        for o in sorted(range(1, NR), key=lambda o: abs(o - NR // 2))
    ]

    n0, n1, n2 = iwv[0:1, :], iwv[1:2, :], iwv[2:3, :]
    n_waves = iwv.shape[1]
    flip = n0 < 0
    n1 = jnp.where(flip, -n1, n1)
    n2 = jnp.where(flip, -n2, n2)
    s1 = jnp.where(n1 < 0, -1.0, 1.0)
    s2 = jnp.where(n2 < 0, -1.0, 1.0)
    place = jnp.abs(n1) * 8 + jnp.abs(n2)
    rows128 = lax.broadcasted_iota(jnp.int32, (128, n_waves), 0)
    hot = jnp.where((rows128 & 63) == place, 1.0, 0.0).astype(BF16)
    mine = lax.broadcasted_iota(jnp.int32, (8, n_waves), 0) == jnp.abs(n0)
    coeffs = [jnp.ones_like(s1), s1, s2, s1 * s2]
    listed = jnp.concatenate([jnp.where(mine, cf, 0.0) for cf in coeffs], axis=0).astype(BF16)
    cnt = nt(listed, hot)
    d_row = lax.broadcasted_iota(jnp.int32, (8, 128), 0)
    l_row = lax.broadcasted_iota(jnp.int32, (8, 128), 1)
    b_row = (l_row & 63) >> 3
    g_row = l_row & 7
    norm2 = jnp.maximum(d_row * d_row + b_row * b_row + g_row * g_row, 1).astype(F32)
    kw = ewald_scale * jnp.exp(-ewald_damp * norm2) / norm2
    for t in range(4):
        wt[t] = cnt[t * 8 : (t + 1) * 8] * kw
    store(3, wt, wt_hbm)

    for cp in loads[4:]:
        cp.wait()
    for cp in vh:
        cp.wait_recv()

    @pl.loop(0, NB)
    def _(g):
        acc = jnp.zeros((400, BS), F32)
        for j in range(NNB):
            i = listed_at(nbr, g, j, first - 2, NB + 3)
            acc += nn(v2[i].reshape(400, BS), ps[g, j])
        ob[:, :, pl.ds(pl.multiple_of(g * BS, BS), BS)] = (acc * rden[g]).astype(BF16).reshape(25, 16, BS)

    store(4, ob, att_hbm)

    for cp in fsend:
        cp.wait_recv()
    gt[inner, gid] = jnp.sum(os_[...], axis=0)
    tsend = [
        send(gt.at[inner, gid], gt.at[inner, gid], t_s.at[o - 1], t_r.at[o - 1], group_peer(o)[1])
        for o in range(1, NG)
    ]
    for cp in tsend:
        cp.wait_recv()
    gsend = [send(gt.at[inner], gt.at[inner], g_s.at[o - 1], g_r.at[o - 1], x_peer(o)) for o in range(1, NX)]
    store(5, gt.at[inner], gt_hbm.at[inner])
    gon = [send(gt.at[inner], gt.at[inner], gf_s.at[0], gf_r.at[0], other)]
    for o in range(1, NX):
        gsend[o - 1].wait_recv()
        got = gt.at[x_from(o)]
        gon.append(send(got, got, gf_s.at[o], gf_r.at[o], other))
        store(5 + o, got, gt_hbm.at[x_from(o)])
    for o, cp in enumerate(gon):
        cp.wait_recv()
        away = x_from(o) + 1 - 2 * c
        store(9 + o, gt.at[away], gt_hbm.at[away])
    for cp in kh + cws + vh + out0 + on0 + out1 + on1 + out2 + on2 + rsend + fsend + tsend + gsend + gon:
        cp.wait_send()
    for cp in stored:
        cp.wait()


def field(
    att_hbm, gt_hbm, wt_hbm, xt_hbm, bt_hbm, chg_hbm, o_att, o_pot, o_for, att, gt, wt, xt, bt, chg, hs, sem
):
    pairs = ((gt_hbm, gt), (wt_hbm, wt), (bt_hbm, bt), (xt_hbm, xt), (chg_hbm, chg), (att_hbm, att))
    takes = [pltpu.make_async_copy(a, b, sem.at[i]) for i, (a, b) in enumerate(pairs)]
    for cp in takes:
        cp.start()
    for cp in takes[:2]:
        cp.wait()

    lane = lax.broadcasted_iota(jnp.int32, (1, 128), 1)
    sgn = jnp.where(lane < 64, -1.0, 1.0)
    w_n1 = ((lane & 63) >> 3).astype(F32)
    w_n2 = (lane & 7).astype(F32)

    def swap(a):
        return pltpu.roll(a, 64, 1)

    for d in range(NI):
        w0, w1, w2, w12 = (wt[t, d : d + 1, :] for t in range(4))
        g4 = {
            (p, u): jnp.concatenate([gt[d, 4 * p + u], gt[d, 4 * p + 2 + u]], axis=0)
            for p in range(2)
            for u in range(2)
        }
        h = {}
        for p in range(2):
            for u in range(2):
                su = sgn if u == 0 else -sgn
                sp = sgn if p == 0 else -sgn
                pu = -1.0 if p == u else 1.0
                h[p, u] = (
                    w0 * g4[p, u]
                    + (su * w12) * swap(g4[p, 1 - u])
                    + (pu * w1) * g4[1 - p, 1 - u]
                    + (sp * w2) * swap(g4[1 - p, u])
                )
        for p in range(2):
            r = p * 16
            hs[d, r : r + 16, 0:128] = h[p, 0].astype(BF16)
            hs[d, r : r + 16, 128:256] = h[p, 1].astype(BF16)
            hs[d, 32 + r : 48 + r, 0:128] = (-w_n1 * h[p, 1]).astype(BF16)
            hs[d, 32 + r : 48 + r, 128:256] = (w_n1 * h[p, 0]).astype(BF16)
            for u in range(2):
                hs[d, 64 + r : 80 + r, u * 128 : u * 128 + 128] = (
                    (w_n2 * sgn) * swap(h[p, u])
                ).astype(BF16)

    for cp in takes[2:5]:
        cp.wait()

    def part(t):
        cols = pl.ds(pl.multiple_of(t * BS, BS), BS)
        basis = bt[:, cols]
        pot = jnp.zeros((16, BS), F32)
        fx = jnp.zeros((16, BS), F32)
        fy = jnp.zeros((16, BS), F32)
        fz = jnp.zeros((16, BS), F32)
        every = nn(hs[...].reshape(NI * 96, 256), basis)
        for d in range(NI):
            r = every[d * 96 : (d + 1) * 96]
            xc = xt[0, d : d + 1, cols]
            xs = xt[1, d : d + 1, cols]
            pot += xc * r[0:16] + xs * r[16:32]
            if d:
                fx += (d * xs) * r[0:16] - (d * xc) * r[16:32]
            fy += xc * r[32:48] + xs * r[48:64]
            fz += xc * r[64:80] + xs * r[80:96]
        o_pot[:, cols] = pot
        ch = chg[:, cols]
        for i, f in enumerate((fx, fy, fz)):
            o_for[i : i + 1, cols] = jnp.sum(ch * f, axis=0, keepdims=True)

    pl.loop(0, 2, unroll=2)(part)
    takes[5].wait()
    give = pltpu.make_async_copy(att, o_att, sem.at[6])
    give.start()
    pl.loop(2, NB, unroll=2)(part)
    give.wait()


def local(queries, key_states, value_states, fractional, block_counts, neighbors, integer_wave_vectors, charge_weight):
    n_atoms = queries.shape[2]
    vmem = pl.BlockSpec(memory_space=pltpu.VMEM)
    hbm = pl.BlockSpec(memory_space=pltpu.HBM)
    dma = pltpu.SemaphoreType.DMA
    att_shape = jax.ShapeDtypeStruct((25, 16, n_atoms), BF16)
    passed = (
        jax.ShapeDtypeStruct((NI, NG, 8, 128), F32),
        jax.ShapeDtypeStruct((4, 8, 128), F32),
        jax.ShapeDtypeStruct((2, 8, n_atoms), F32),
        jax.ShapeDtypeStruct((256, n_atoms), BF16),
        jax.ShapeDtypeStruct((16, n_atoms), F32),
    )
    slots = [pltpu.VMEM(t.shape, t.dtype) for t in passed]
    made = pl.pallas_call(
        kernel,
        out_shape=(att_shape,) + passed,
        in_specs=[hbm] * 8,
        out_specs=(hbm,) * 6,
        scratch_shapes=[pltpu.VMEM(att_shape.shape, BF16)]
        + slots
        + [
            dma((13,)),
            pltpu.VMEM((1, 16, n_atoms), BF16),
            pltpu.VMEM((1, 16, n_atoms), BF16),
            pltpu.VMEM((3, n_atoms), F32),
            pltpu.SMEM(block_counts.shape, jnp.int32),
            pltpu.SMEM((NNB, NB), jnp.int32),
            pltpu.VMEM(integer_wave_vectors.shape, jnp.int32),
            pltpu.VMEM((16, 16), BF16),
            dma((7,)),
            pltpu.VMEM((NB + 4, 25, 16, BS), BF16),
            pltpu.VMEM((16, n_atoms), BF16),
            pltpu.VMEM((NB, 48, BS), BF16),
            pltpu.VMEM((4, 48, BS), BF16),
            pltpu.VMEM((NB + 4, 48, BS), BF16),
            pltpu.VMEM((NB, 32, BS), BF16),
            pltpu.VMEM((NB, NNB, BS, BS), BF16),
            pltpu.VMEM((NB, 1, BS), F32),
            pltpu.VMEM((NI, NB, 16, BS), BF16),
            pltpu.VMEM((NI, 16, 16), BF16),
            pltpu.VMEM((NG, 8, 128), F32),
            pltpu.VMEM((NG, 8, 128), F32),
            pltpu.VMEM((NR, 8, 128), F32),
            dma((NB,)),
            dma,
            pltpu.SemaphoreType.REGULAR((3,)),
            dma((4,)),
            dma((4,)),
            dma((3, NX - 1)),
            dma((3, NX - 1)),
            dma((3, NX)),
            dma((3, NX)),
            dma((NI - 1,)),
            dma((NI - 1,)),
            dma((NG - 1,)),
            dma((NG - 1,)),
            dma((NR - 1,)),
            dma((NR - 1,)),
            dma((NG - 1,)),
            dma((NG - 1,)),
            dma((NX - 1,)),
            dma((NX - 1,)),
            dma((NX,)),
            dma((NX,)),
        ],
        compiler_params=pltpu.CompilerParams(
            collective_id=0, has_side_effects=True, vmem_limit_bytes=56 << 20
        ),
    )(
        queries,
        key_states,
        fractional,
        block_counts,
        neighbors.T,
        integer_wave_vectors,
        charge_weight,
        value_states.transpose(1, 0, 2),
    )
    attention, potential, forces = pl.pallas_call(
        field,
        out_shape=(
            att_shape,
            jax.ShapeDtypeStruct((16, n_atoms), F32),
            jax.ShapeDtypeStruct((3, n_atoms), F32),
        ),
        in_specs=[hbm] * 6,
        out_specs=(hbm, vmem, vmem),
        scratch_shapes=[pltpu.VMEM(att_shape.shape, BF16)]
        + slots
        + [pltpu.VMEM((NI, 96, 256), BF16), dma((7,))],
        compiler_params=pltpu.CompilerParams(vmem_limit_bytes=56 << 20),
    )(*made)
    return attention.transpose(1, 0, 2), potential, forces


def solution(mesh):
    torus = Mesh(mesh.devices.reshape(NY, NZ, NX, NC), ("y", "z", "x", "c"))
    return jax.shard_map(
        local,
        mesh=torus,
        in_specs=(
            P(INNER, None, SEQ),
            P(INNER, None, SEQ),
            P(INNER, None, SEQ),
            P(None, SEQ),
            P(),
            P(SEQ, None),
            P(),
            P(INNER, None),
        ),
        out_specs=(P(INNER, None, SEQ), P(None, SEQ), P(None, SEQ)),
        check_vma=False,
    )
```

```python
import jax
import jax.numpy as jnp
from jax import lax
from jax.experimental import pallas as pl
from jax.experimental.pallas import tpu as pltpu
from jax.sharding import Mesh
from jax.sharding import PartitionSpec as P

BS = 256
NNB = 3
NY, NZ, NX, NC = 4, 32, 4, 2
SEQ = ("y", "z")
INNER = ("x", "c")
NI = NX * NC
NSEQ = NY * NZ
GZ = 2
NG = NY * GZ
NR = NZ // GZ
NB = 8
F32, BF16 = jnp.float32, jnp.bfloat16
MESH = pl.DeviceIdType.MESH
DEAD = -1e30

ewald_scale = 40.0
ewald_damp = 0.02

COS = (1.0, -19.739208221435547, 64.93939208984375, -85.45665740966797, 60.242130279541016, -26.4046688079834, 7.800131320953369, -1.4531123638153076)
SIN = (6.2831854820251465, -41.34170150756836, 81.6052474975586, -76.70575714111328, 42.057369232177734, -15.084554672241211, 3.7759575843811035, -0.6150599718093872)


def poly(coeffs, u):
    y = jnp.full_like(u, coeffs[-1])
    for k in coeffs[-2::-1]:
        y = y * u + k
    return y


def cos_sin_turns(t):
    r = t - jnp.floor(t + 0.5)
    u = r * r
    return poly(COS, u), poly(SIN, u) * r


def nt(a, b):
    return lax.dot_general(a, b, (((1,), (1,)), ((), ())), preferred_element_type=F32)


def tn(a, b):
    return lax.dot_general(a, b, (((0,), (0,)), ((), ())), preferred_element_type=F32)


def nn(a, b):
    return jnp.dot(a, b, preferred_element_type=F32)


def listed_at(nbr, g, j, low, high):
    return jnp.clip(nbr[j, g] - low, 0, high)


def kernel(
    q_hbm, k_hbm, frac_hbm, counts_hbm, nbr_hbm, iwv_hbm, cw_hbm, v_hbm,
    att_hbm, gt_hbm, wt_hbm, xt_hbm, bt_hbm, chg_hbm,
    ob, gt, wt, xt, bt, chg, sem_o,
    q, k, frac, counts, nbr, iwv, cw, sem_i, v2, v0, ks, kin, kb, qs, ps, rden, a0, cwa, gs, rs, os_,
    sem_v, sem_v0, known, halo_s, halo_r, a_s, a_r, af_s, af_r, c_s, c_r, r_s, r_r, f_s, f_r, t_s, t_r, g_s, g_r, gf_s, gf_r,
):
    y, z, x, c = (lax.axis_index(a) for a in ("y", "z", "x", "c"))
    inner = x * NC + c
    seq = y * NZ + z
    gid = y * GZ + lax.rem(z, GZ)
    rid = z // GZ
    first = seq * NB

    def at_seq(s):
        return {"y": s // NZ, "z": lax.rem(s, NZ)}

    right = at_seq(lax.rem(seq + 1, NSEQ))
    left = at_seq(lax.rem(seq + NSEQ - 1, NSEQ))
    other = {"c": 1 - c}

    def inner_peer(o):
        p = lax.rem(inner + o, NI)
        return {"x": p // NC, "c": lax.rem(p, NC)}

    def x_peer(o):
        return {"x": lax.rem(x + o, NX)}

    def x_from(o):
        return lax.rem(x + NX - o, NX) * NC + c

    def group_peer(o):
        p = lax.rem(gid + o, NG)
        return p, {"y": p // GZ, "z": rid * GZ + lax.rem(p, GZ)}

    def ring_peer(o):
        p = lax.rem(rid + o, NR)
        return {"z": p * GZ + lax.rem(z, GZ)}

    pairs = ((k_hbm, k), (counts_hbm, counts), (q_hbm, q), (cw_hbm, cw), (nbr_hbm, nbr), (frac_hbm, frac), (iwv_hbm, iwv))
    takes = [pltpu.make_async_copy(a, b, sem_i.at[i]) for i, (a, b) in enumerate(pairs)]
    load_v0 = pltpu.make_async_copy(v_hbm.at[0], v0, sem_v0)
    for cp in takes[:2] + [load_v0] + takes[2:]:
        cp.start()

    barrier = pltpu.get_barrier_semaphore()
    near = [left, right, ring_peer(1), ring_peer(NR - 1)]
    near += [inner_peer(o) for o in range(1, NI)]
    near += [group_peer(o)[1] for o in range(1, NG)]
    for p in near:
        pl.semaphore_signal(barrier, inc=1, device_id=p, device_id_type=MESH)

    def tell(r):
        for o in (1 << r, NR - (1 << r)):
            pl.semaphore_signal(known.at[r], inc=1, device_id=ring_peer(o), device_id_type=MESH)

    def hear(r):
        pl.semaphore_wait(known.at[r], 2)

    loads = []
    for b in (0, 1, 6, 7, 2, 3, 4, 5):
        cp = pltpu.make_async_copy(v_hbm.at[:, :, pl.ds(b * BS, BS)], v2.at[b + 2], sem_v.at[b])
        cp.start()
        loads.append(cp)

    for cp in takes[:2]:
        cp.wait()

    row16 = lax.broadcasted_iota(jnp.int32, (16, BS), 0)
    lane16 = lax.broadcasted_iota(jnp.int32, (16, BS), 1)
    def build(b):
        cols = pl.ds(b * BS, BS)
        live = lane16 < counts[first + b]
        bias = jnp.where((row16 == 0) & jnp.logical_not(live), DEAD, 0.0)
        ks[b, 0:16, :] = k[0, :, cols]
        ks[b, 16:32, :] = bias.astype(BF16)
        ks[b, 32:48, :] = v0[:, b * BS : (b + 1) * BS]

    load_v0.wait()
    for b in (0, 1, 6, 7):
        build(b)

    def send(src, dst, ssem, rsem, dev):
        cp = pltpu.make_async_remote_copy(
            src_ref=src, dst_ref=dst, send_sem=ssem, recv_sem=rsem, device_id=dev, device_id_type=MESH
        )
        cp.start()
        return cp

    pl.semaphore_wait(barrier, len(near))
    kh = [
        send(ks.at[pl.ds(6, 2)], kin.at[pl.ds(0, 2)], halo_s.at[0], halo_r.at[0], right),
        send(ks.at[pl.ds(0, 2)], kin.at[pl.ds(2, 2)], halo_s.at[1], halo_r.at[1], left),
    ]
    tell(0)
    for cp in takes[2:5]:
        cp.wait()
    cwa[inner] = cw[...]
    cws = [
        send(cwa.at[inner], cwa.at[inner], c_s.at[o - 1], c_r.at[o - 1], inner_peer(o))
        for o in range(1, NI)
    ]
    for b in (2, 3, 4, 5):
        build(b)
    for b in range(NB):
        qs[b, 0:16, :] = (q[0, :, b * BS : (b + 1) * BS].astype(F32) * 0.25).astype(BF16)
        qs[b, 16:32, :] = jnp.where(row16 == 0, 1.0, 0.0).astype(BF16)
    for cp in loads[:4]:
        cp.wait()
    vh = [
        send(v2.at[pl.ds(8, 2)], v2.at[pl.ds(0, 2)], halo_s.at[2], halo_r.at[2], right),
        send(v2.at[pl.ds(2, 2)], v2.at[pl.ds(10, 2)], halo_s.at[3], halo_r.at[3], left),
    ]

    def attend(src, low, high, at):
        g = lax.rem(at + 2, NB)
        listed = [listed_at(nbr, g, j, low, high) for j in range(NNB)]
        qa = qs[g]
        s = [tn(src[i, 0:32, :], qa) for i in listed]
        m = s[0].max(axis=0, keepdims=True)
        for t in s[1:]:
            m = jnp.maximum(m, t.max(axis=0, keepdims=True))
        den = jnp.zeros((1, BS), F32)
        acc = jnp.zeros((16, BS), F32)
        for j, i in enumerate(listed):
            w = jnp.exp(s[j] - m)
            den += w.sum(axis=0, keepdims=True)
            wb = w.astype(BF16)
            ps[g, j] = wb
            acc += nn(src[i, 32:48, :], wb)
        live_q = lax.broadcasted_iota(jnp.int32, (1, BS), 1) < counts[first + g]
        rd = jnp.where(live_q, 1.0 / den, 0.0)
        rden[g] = rd
        a0[inner, at] = (acc * rd).astype(BF16)

    pieces = (pl.ds(0, 4), pl.ds(4, 2), pl.ds(6, 2))

    def spread(i):
        mine = a0.at[inner, pieces[i]]
        out = [send(mine, mine, a_s.at[i, o - 1], a_r.at[i, o - 1], x_peer(o)) for o in range(1, NX)]
        return out, [send(mine, mine, af_s.at[i, 0], af_r.at[i, 0], other)]

    def pass_on(i, out, on):
        for o in range(1, NX):
            out[o - 1].wait_recv()
            got = a0.at[x_from(o), pieces[i]]
            on.append(send(got, got, af_s.at[i, o], af_r.at[i, o], other))

    @pl.loop(0, 4, unroll=2)
    def _(at):
        attend(ks, first, NB - 1, at)

    out0, on0 = spread(0)
    for cp in kh:
        cp.wait_recv()
    hear(0)
    tell(1)
    kb[0:2] = kin[0:2]
    kb[2:10] = ks[...]
    kb[10:12] = kin[2:4]

    @pl.loop(4, 6, unroll=2)
    def _(at):
        attend(kb, first - 2, NB + 3, at)

    out1, on1 = spread(1)

    @pl.loop(6, 8, unroll=2)
    def _(at):
        attend(kb, first - 2, NB + 3, at)

    out2, on2 = spread(2)
    pass_on(0, out0, on0)
    hear(1)
    tell(2)

    for cp in takes[5:]:
        cp.wait()

    n_atoms = NB * BS
    iota8 = lax.broadcasted_iota(jnp.int32, (8, n_atoms), 0).astype(F32)
    xc, xs = cos_sin_turns(frac[0:1, :] * iota8)
    xt[0] = xc
    xt[1] = xs
    u_tab = cos_sin_turns(frac[1:2, :] * iota8)
    v_tab = cos_sin_turns(frac[2:3, :] * iota8)
    for u in range(2):
        for v in range(2):
            for n in range(0, 8, 2):
                lo = u_tab[u][n : n + 1, :] * v_tab[v]
                hi = u_tab[u][n + 1 : n + 2, :] * v_tab[v]
                at = u * 128 + v * 64 + n * 8
                bt[at : at + 16, :] = jnp.concatenate([lo, hi], axis=0).astype(BF16)

    stored = []

    def store(i, src, dst):
        cp = pltpu.make_async_copy(src, dst, sem_o.at[i])
        cp.start()
        stored.append(cp)

    store(0, bt, bt_hbm)
    store(1, xt, xt_hbm)

    def charge(at):
        g = (at + 2) % NB
        r = tn(cwa[...].reshape(NI * 16, 16), a0[:, at].reshape(NI * 16, BS))
        chg[:, g * BS : (g + 1) * BS] = r

    def structure(low, high):
        cols = slice(low * BS, high * BS)
        charges = chg[:, cols]
        own_c = xt[0, pl.ds(inner, 1), cols]
        own_s = xt[1, pl.ds(inner, 1), cols]
        amp = jnp.concatenate([charges * own_c, charges * own_s], axis=0) * (1.0 / 512.0)
        amp_h = amp.astype(BF16)
        amp_l = (amp - amp_h.astype(F32)).astype(BF16)
        both = nt(jnp.concatenate([amp_h, amp_l], axis=0), bt[:, cols])
        return both[0:32] + both[32:64]

    for cp in cws + on0:
        cp.wait_recv()
    for at in range(4):
        charge(at)
    part = structure(2, 6)
    pass_on(1, out1, on1)
    pass_on(2, out2, on2)
    for cp in on1 + on2:
        cp.wait_recv()
    for at in range(4, 8):
        charge(at)
    part += structure(0, 2) + structure(6, 8)
    store(2, chg, chg_hbm)
    for p in range(8):
        gs[p] = part[(p // 2) * 8 : (p // 2) * 8 + 8, (p % 2) * 128 : (p % 2) * 128 + 128]

    rsend = []
    for o in range(1, NG):
        p, dev = group_peer(o)
        rsend.append(send(gs.at[p], rs.at[gid], r_s.at[o - 1], r_r.at[o - 1], dev))
    rs[gid] = gs[gid]
    hear(2)
    for cp in rsend:
        cp.wait_recv()
    os_[rid] = jnp.sum(rs[...], axis=0)
    fsend = [
        send(os_.at[rid], os_.at[rid], f_s.at[o - 1], f_r.at[o - 1], ring_peer(o))
        for o in sorted(range(1, NR), key=lambda o: abs(o - NR // 2))
    ]

    n0, n1, n2 = iwv[0:1, :], iwv[1:2, :], iwv[2:3, :]
    n_waves = iwv.shape[1]
    flip = n0 < 0
    n1 = jnp.where(flip, -n1, n1)
    n2 = jnp.where(flip, -n2, n2)
    s1 = jnp.where(n1 < 0, -1.0, 1.0)
    s2 = jnp.where(n2 < 0, -1.0, 1.0)
    place = jnp.abs(n1) * 8 + jnp.abs(n2)
    rows128 = lax.broadcasted_iota(jnp.int32, (128, n_waves), 0)
    hot = jnp.where((rows128 & 63) == place, 1.0, 0.0).astype(BF16)
    mine = lax.broadcasted_iota(jnp.int32, (8, n_waves), 0) == jnp.abs(n0)
    coeffs = [jnp.ones_like(s1), s1, s2, s1 * s2]
    listed = jnp.concatenate([jnp.where(mine, cf, 0.0) for cf in coeffs], axis=0).astype(BF16)
    cnt = nt(listed, hot)
    d_row = lax.broadcasted_iota(jnp.int32, (8, 128), 0)
    l_row = lax.broadcasted_iota(jnp.int32, (8, 128), 1)
    b_row = (l_row & 63) >> 3
    g_row = l_row & 7
    norm2 = jnp.maximum(d_row * d_row + b_row * b_row + g_row * g_row, 1).astype(F32)
    kw = ewald_scale * jnp.exp(-ewald_damp * norm2) / norm2
    for t in range(4):
        wt[t] = cnt[t * 8 : (t + 1) * 8] * kw
    store(3, wt, wt_hbm)

    for cp in loads[4:]:
        cp.wait()
    for cp in vh:
        cp.wait_recv()

    @pl.loop(0, NB)
    def _(g):
        acc = jnp.zeros((400, BS), F32)
        for j in range(NNB):
            i = listed_at(nbr, g, j, first - 2, NB + 3)
            acc += nn(v2[i].reshape(400, BS), ps[g, j])
        ob[:, :, pl.ds(pl.multiple_of(g * BS, BS), BS)] = (acc * rden[g]).astype(BF16).reshape(25, 16, BS)

    store(4, ob, att_hbm)

    for cp in fsend:
        cp.wait_recv()
    gt[inner, gid] = jnp.sum(os_[...], axis=0)
    tsend = [
        send(gt.at[inner, gid], gt.at[inner, gid], t_s.at[o - 1], t_r.at[o - 1], group_peer(o)[1])
        for o in range(1, NG)
    ]
    gsend = []
    for i in range(NG):
        if i:
            tsend[i - 1].wait_recv()
        got = gt.at[inner, lax.rem(gid + NG - i, NG)]
        gsend.append([send(got, got, g_s.at[i, o - 1], g_r.at[i, o - 1], x_peer(o)) for o in range(1, NX)])
    store(5, gt.at[inner], gt_hbm.at[inner])
    gon = [send(gt.at[inner], gt.at[inner], gf_s.at[0], gf_r.at[0], other)]
    for o in range(1, NX):
        for sent in gsend:
            sent[o - 1].wait_recv()
        got = gt.at[x_from(o)]
        gon.append(send(got, got, gf_s.at[o], gf_r.at[o], other))
        store(5 + o, got, gt_hbm.at[x_from(o)])
    for o, cp in enumerate(gon):
        cp.wait_recv()
        away = x_from(o) + 1 - 2 * c
        store(9 + o, gt.at[away], gt_hbm.at[away])
    for cp in kh + cws + vh + out0 + on0 + out1 + on1 + out2 + on2 + rsend + fsend + tsend + sum(gsend, []) + gon:
        cp.wait_send()
    for cp in stored:
        cp.wait()


def field(
    att_hbm, gt_hbm, wt_hbm, xt_hbm, bt_hbm, chg_hbm, o_att, o_pot, o_for, att, gt, wt, xt, bt, chg, hs, sem
):
    pairs = ((gt_hbm, gt), (wt_hbm, wt), (bt_hbm, bt), (xt_hbm, xt), (chg_hbm, chg), (att_hbm, att))
    takes = [pltpu.make_async_copy(a, b, sem.at[i]) for i, (a, b) in enumerate(pairs)]
    for cp in takes:
        cp.start()
    for cp in takes[:2]:
        cp.wait()

    lane = lax.broadcasted_iota(jnp.int32, (1, 128), 1)
    sgn = jnp.where(lane < 64, -1.0, 1.0)
    w_n1 = ((lane & 63) >> 3).astype(F32)
    w_n2 = (lane & 7).astype(F32)

    def swap(a):
        return pltpu.roll(a, 64, 1)

    for d in range(NI):
        w0, w1, w2, w12 = (wt[t, d : d + 1, :] for t in range(4))
        g4 = {
            (p, u): jnp.concatenate([gt[d, 4 * p + u], gt[d, 4 * p + 2 + u]], axis=0)
            for p in range(2)
            for u in range(2)
        }
        h = {}
        for p in range(2):
            for u in range(2):
                su = sgn if u == 0 else -sgn
                sp = sgn if p == 0 else -sgn
                pu = -1.0 if p == u else 1.0
                h[p, u] = (
                    w0 * g4[p, u]
                    + (su * w12) * swap(g4[p, 1 - u])
                    + (pu * w1) * g4[1 - p, 1 - u]
                    + (sp * w2) * swap(g4[1 - p, u])
                )
        for p in range(2):
            r = p * 16
            hs[d, r : r + 16, 0:128] = h[p, 0].astype(BF16)
            hs[d, r : r + 16, 128:256] = h[p, 1].astype(BF16)
            hs[d, 32 + r : 48 + r, 0:128] = (-w_n1 * h[p, 1]).astype(BF16)
            hs[d, 32 + r : 48 + r, 128:256] = (w_n1 * h[p, 0]).astype(BF16)
            for u in range(2):
                hs[d, 64 + r : 80 + r, u * 128 : u * 128 + 128] = (
                    (w_n2 * sgn) * swap(h[p, u])
                ).astype(BF16)

    for cp in takes[2:5]:
        cp.wait()

    def part(t):
        cols = pl.ds(pl.multiple_of(t * BS, BS), BS)
        basis = bt[:, cols]
        pot = jnp.zeros((16, BS), F32)
        fx = jnp.zeros((16, BS), F32)
        fy = jnp.zeros((16, BS), F32)
        fz = jnp.zeros((16, BS), F32)
        every = nn(hs[...].reshape(NI * 96, 256), basis)
        for d in range(NI):
            r = every[d * 96 : (d + 1) * 96]
            xc = xt[0, d : d + 1, cols]
            xs = xt[1, d : d + 1, cols]
            pot += xc * r[0:16] + xs * r[16:32]
            if d:
                fx += (d * xs) * r[0:16] - (d * xc) * r[16:32]
            fy += xc * r[32:48] + xs * r[48:64]
            fz += xc * r[64:80] + xs * r[80:96]
        o_pot[:, cols] = pot
        ch = chg[:, cols]
        for i, f in enumerate((fx, fy, fz)):
            o_for[i : i + 1, cols] = jnp.sum(ch * f, axis=0, keepdims=True)

    pl.loop(0, 2, unroll=2)(part)
    takes[5].wait()
    give = pltpu.make_async_copy(att, o_att, sem.at[6])
    give.start()
    pl.loop(2, NB, unroll=2)(part)
    give.wait()


def local(queries, key_states, value_states, fractional, block_counts, neighbors, integer_wave_vectors, charge_weight):
    n_atoms = queries.shape[2]
    vmem = pl.BlockSpec(memory_space=pltpu.VMEM)
    hbm = pl.BlockSpec(memory_space=pltpu.HBM)
    dma = pltpu.SemaphoreType.DMA
    att_shape = jax.ShapeDtypeStruct((25, 16, n_atoms), BF16)
    passed = (
        jax.ShapeDtypeStruct((NI, NG, 8, 128), F32),
        jax.ShapeDtypeStruct((4, 8, 128), F32),
        jax.ShapeDtypeStruct((2, 8, n_atoms), F32),
        jax.ShapeDtypeStruct((256, n_atoms), BF16),
        jax.ShapeDtypeStruct((16, n_atoms), F32),
    )
    slots = [pltpu.VMEM(t.shape, t.dtype) for t in passed]
    made = pl.pallas_call(
        kernel,
        out_shape=(att_shape,) + passed,
        in_specs=[hbm] * 8,
        out_specs=(hbm,) * 6,
        scratch_shapes=[pltpu.VMEM(att_shape.shape, BF16)]
        + slots
        + [
            dma((13,)),
            pltpu.VMEM((1, 16, n_atoms), BF16),
            pltpu.VMEM((1, 16, n_atoms), BF16),
            pltpu.VMEM((3, n_atoms), F32),
            pltpu.SMEM(block_counts.shape, jnp.int32),
            pltpu.SMEM((NNB, NB), jnp.int32),
            pltpu.VMEM(integer_wave_vectors.shape, jnp.int32),
            pltpu.VMEM((16, 16), BF16),
            dma((7,)),
            pltpu.VMEM((NB + 4, 25, 16, BS), BF16),
            pltpu.VMEM((16, n_atoms), BF16),
            pltpu.VMEM((NB, 48, BS), BF16),
            pltpu.VMEM((4, 48, BS), BF16),
            pltpu.VMEM((NB + 4, 48, BS), BF16),
            pltpu.VMEM((NB, 32, BS), BF16),
            pltpu.VMEM((NB, NNB, BS, BS), BF16),
            pltpu.VMEM((NB, 1, BS), F32),
            pltpu.VMEM((NI, NB, 16, BS), BF16),
            pltpu.VMEM((NI, 16, 16), BF16),
            pltpu.VMEM((NG, 8, 128), F32),
            pltpu.VMEM((NG, 8, 128), F32),
            pltpu.VMEM((NR, 8, 128), F32),
            dma((NB,)),
            dma,
            pltpu.SemaphoreType.REGULAR((3,)),
            dma((4,)),
            dma((4,)),
            dma((3, NX - 1)),
            dma((3, NX - 1)),
            dma((3, NX)),
            dma((3, NX)),
            dma((NI - 1,)),
            dma((NI - 1,)),
            dma((NG - 1,)),
            dma((NG - 1,)),
            dma((NR - 1,)),
            dma((NR - 1,)),
            dma((NG - 1,)),
            dma((NG - 1,)),
            dma((NG, NX - 1)),
            dma((NG, NX - 1)),
            dma((NX,)),
            dma((NX,)),
        ],
        compiler_params=pltpu.CompilerParams(
            collective_id=0, has_side_effects=True, vmem_limit_bytes=56 << 20
        ),
    )(
        queries,
        key_states,
        fractional,
        block_counts,
        neighbors.T,
        integer_wave_vectors,
        charge_weight,
        value_states.transpose(1, 0, 2),
    )
    attention, potential, forces = pl.pallas_call(
        field,
        out_shape=(
            att_shape,
            jax.ShapeDtypeStruct((16, n_atoms), F32),
            jax.ShapeDtypeStruct((3, n_atoms), F32),
        ),
        in_specs=[hbm] * 6,
        out_specs=(hbm, vmem, vmem),
        scratch_shapes=[pltpu.VMEM(att_shape.shape, BF16)]
        + slots
        + [pltpu.VMEM((NI, 96, 256), BF16), dma((7,))],
        compiler_params=pltpu.CompilerParams(vmem_limit_bytes=56 << 20),
    )(*made)
    return attention.transpose(1, 0, 2), potential, forces


def solution(mesh):
    torus = Mesh(mesh.devices.reshape(NY, NZ, NX, NC), ("y", "z", "x", "c"))
    return jax.shard_map(
        local,
        mesh=torus,
        in_specs=(
            P(INNER, None, SEQ),
            P(INNER, None, SEQ),
            P(INNER, None, SEQ),
            P(None, SEQ),
            P(),
            P(SEQ, None),
            P(),
            P(INNER, None),
        ),
        out_specs=(P(INNER, None, SEQ), P(None, SEQ), P(None, SEQ)),
        check_vma=False,
    )
```
